256 devices in a mesh: dp: 32 (over y, z), tensor: 8 (over x, core).
Axes of the slice: x: 4, y: 4, z: 8, core: 2. Of those that a mesh axis runs over, the one named last changes fastest.
Arguments:
- layer_inputs: bfloat16 [4096, 4, 1024], P('dp', None, 'tensor'), may hold values from -125 to 125
- output_grads: bfloat16 [4096, 10240], P('dp'), may hold values from -0.0109375 to 0.0109375
- left_stats: float32 [32, 2, 1024, 1024], P('dp', None, 'tensor'), may hold values from -6 to 6
- right_stats: float32 [32, 2, 1024, 1024], P('dp', None, 'tensor'), may hold values from -6 to 6
- left_roots: bfloat16 [32, 2, 1024, 1024], P('dp', None, 'tensor'), may hold values from -0.2 to 7.2
- right_roots: bfloat16 [32, 2, 1024, 1024], P('dp'), may hold values from -0.2 to 2.2
- owner_blocks: int32 [32, 2], replicated, may hold values from -1 to 39, as said below
- block_counts: int32 [32], replicated, may hold values from 0 to 2, as said below
Outputs:
- new_left: float32 [32, 2, 1024, 1024], P('dp', None, 'tensor')
- new_right: float32 [32, 2, 1024, 1024], P('dp', None, 'tensor')
- grafted_update: bfloat16 [1024, 4, 10240], P(('tensor', 'dp'))
The draws below stay inside these ranges and needn't reach their ends.
Inputs may be any that keep to these rules, and one draw needn't show every extreme that they name: `owner_blocks`: row o lists, in slots 0 to block_counts[o] - 1, the blocks that dp index o owns, numbered i * 10 + j for block row i and block column j; every block is listed exactly once over all rows; the other slots hold -1; some owner lists 2 blocks. `block_counts`: number of blocks of each owner; they sum to 40.
All inputs are finite; a program needn't handle non-finite values.
Results may differ from the reference program's by a relative error of at most 0.025.
Values may be sent and summed in bfloat16 or wider, within the bound.
A program may use at most 128 MiB of HBM per device.

```python
import math
import jax
import jax.numpy as jnp
from jax import lax

BL = 1024
TOK_DEV = 128
C = 10240
TOKENS = 4096
NRB = 4
NCB = 10
NB = 40
MOST = 2
N_DP = 32


def owner_table(key):
    seeded = jax.random.fold_in(key, 901)
    key_full, key_rest, key_perm = jax.random.split(seeded, 3)
    busiest = jax.random.randint(key_full, (), 0, N_DP)
    shuffled = jax.random.permutation(key_rest, (N_DP - 1) * MOST).reshape(N_DP - 1, MOST)
    chosen = shuffled < NB - MOST
    owner_ids = jnp.arange(N_DP, dtype=jnp.int32)
    source = jnp.clip(owner_ids - (owner_ids > busiest).astype(jnp.int32), 0, max(N_DP - 2, 0))
    row_chosen = jnp.where((owner_ids == busiest)[:, None], True, chosen[source])
    counts = jnp.sum(row_chosen.astype(jnp.int32), axis=1)
    alive = jnp.arange(MOST, dtype=jnp.int32)[None, :] < counts[:, None]
    running = jnp.cumsum(alive.reshape(-1).astype(jnp.int32)) - 1
    blocks = jax.random.permutation(key_perm, NB).astype(jnp.int32)
    listing = jnp.where(alive.reshape(-1), blocks[jnp.clip(running, 0, NB - 1)], -1)
    return (listing.reshape(N_DP, MOST).astype(jnp.int32), counts.astype(jnp.int32))


def draw_owner_blocks(key, part):
    listing, counts = owner_table(key)
    return listing


def draw_block_counts(key, part):
    listing, counts = owner_table(key)
    return counts


def draw_layer_inputs(key, part):
    key = jax.random.fold_in(key, 11)
    key_noise, key_scale = jax.random.split(key, 2)
    position = jnp.arange(BL, dtype=jnp.float32) / BL
    spread = jnp.exp(jax.random.uniform(key_scale, (NRB, BL)) * math.log(10.0))
    noise_draw = jnp.clip(jax.random.normal(key_noise, (TOKENS, NRB, BL)), -5.0, 5.0)
    values = noise_draw * spread * (1.0 + 0.75 * position)
    return values.astype(jnp.bfloat16)


def draw_output_grads(key, part):
    key = jax.random.fold_in(key, 23)
    key_noise, key_scale = jax.random.split(key, 2)
    factor = 0.01 * TOKENS ** (-0.5)
    spread = jnp.exp(jax.random.uniform(key_scale, (1, C)) * math.log(10.0))
    noise_draw = jnp.clip(jax.random.normal(key_noise, (TOKENS, C)), -5.0, 5.0)
    values = noise_draw * spread * factor
    return values.astype(jnp.bfloat16)


def draw_left_roots(key, part):
    key = jax.random.fold_in(key, 37)
    key_off, key_diag = jax.random.split(key, 2)
    shape = (N_DP, MOST, BL, BL)
    position = jnp.arange(BL, dtype=jnp.float32) / BL
    offdiag = jnp.clip(jax.random.normal(key_off, shape), -5.0, 5.0) * 0.02
    ramp = 1.0 + 0.75 * position
    offdiag = (offdiag + jnp.swapaxes(offdiag, 2, 3)) * 0.7071
    diagonal = 0.5 * jnp.exp(jax.random.uniform(key_diag, (N_DP, MOST, BL)) * math.log(4.0)) * ramp
    values = offdiag + diagonal[..., None] * jnp.eye(BL, dtype=jnp.float32)
    return values.astype(jnp.bfloat16)


def draw_right_roots(key, part):
    key = jax.random.fold_in(key, 41)
    key_off, key_diag = jax.random.split(key, 2)
    shape = (N_DP, MOST, BL, BL)
    offdiag = jnp.clip(jax.random.normal(key_off, shape), -5.0, 5.0) * 0.02
    offdiag = (offdiag + jnp.swapaxes(offdiag, 2, 3)) * 0.7071
    diagonal = 0.5 * jnp.exp(jax.random.uniform(key_diag, (N_DP, MOST, BL)) * math.log(4.0))
    values = offdiag + diagonal[..., None] * jnp.eye(BL, dtype=jnp.float32)
    return values.astype(jnp.bfloat16)


def block_levels(own_key, shape, pieces, low, top_value):
    level = 1.0
    for axis_at, shards_of in pieces:
        heights = jax.random.uniform(jax.random.fold_in(jax.random.fold_in(own_key, 6), axis_at), (shards_of,), jnp.float32, low / len(pieces), top_value / len(pieces))
        level = level * jnp.repeat(jnp.exp(heights), shape[axis_at] // shards_of).reshape((-1,) + (1,) * (len(shape) - 1 - axis_at))
    return level


def noise(rng, dims, scale, reach, cuts=(), kind=jnp.bfloat16):
    array = scale * jax.random.normal(rng, dims, jnp.float32)
    if cuts:
        array = array * block_levels(rng, dims, cuts, -0.22, 0.18)
    return jnp.clip(array, -reach, reach).astype(kind)


def setup_inputs(seed: int = 0) -> dict:
    keys = jax.random.split(jax.random.key(seed), 9)
    return {
        "layer_inputs": draw_layer_inputs(jax.random.fold_in(keys[8], 71), 0),
        "output_grads": draw_output_grads(jax.random.fold_in(keys[8], 71), 0),
        "left_stats": noise(keys[2], (N_DP, MOST, BL, BL), 1.0, 6.0, ((0, 32), (2, 8)), jnp.float32),
        "right_stats": noise(keys[3], (N_DP, MOST, BL, BL), 1.0, 6.0, ((0, 32), (2, 8)), jnp.float32),
        "left_roots": draw_left_roots(jax.random.fold_in(keys[8], 71), 0),
        "right_roots": draw_right_roots(jax.random.fold_in(keys[8], 71), 0),
        "owner_blocks": draw_owner_blocks(jax.random.fold_in(keys[8], 71), 0),
        "block_counts": draw_block_counts(jax.random.fold_in(keys[8], 71), 0),
    }


decay_rate = 0.99
epsilon = 1e-06

def reference(layer_inputs, output_grads, left_stats, right_stats, left_roots, right_roots, owner_blocks, block_counts):
    inputs_grouped = layer_inputs.reshape(N_DP, TOK_DEV, NRB, BL)
    grads_grouped = output_grads.reshape(N_DP, TOK_DEV, C)

    def accumulate(running, pair):
        inputs_slice, grads_slice = pair
        partial_sum = jnp.einsum('tir,tc->ric', inputs_slice.astype(jnp.float32), grads_slice.astype(jnp.float32))
        rounded = lax.optimization_barrier(partial_sum.astype(jnp.bfloat16))
        return (running + rounded.astype(jnp.float32), 0)
    running, ignored = lax.scan(accumulate, jnp.zeros((BL, NRB, C), jnp.float32), (inputs_grouped, grads_grouped))
    grads = running.astype(jnp.bfloat16)
    blocks_all = grads.reshape(BL, NRB, NCB, BL).transpose(1, 2, 0, 3).reshape(NB, BL, BL)
    slot_total = N_DP * MOST
    live_slots = (jnp.arange(MOST, dtype=jnp.int32)[None, :] < block_counts[:, None]).reshape(-1)
    listed = owner_blocks.reshape(-1)
    matches = (listed[None, :] == jnp.arange(NB, dtype=jnp.int32)[:, None]) & live_slots[None, :]
    slot_of = lax.optimization_barrier(jnp.sum(jnp.where(matches, jnp.arange(slot_total, dtype=jnp.int32)[None, :], 0), axis=1)).astype(jnp.int32)
    left_flat = left_stats.reshape(slot_total, BL, BL)
    right_flat = right_stats.reshape(slot_total, BL, BL)
    left_root_flat = left_roots.reshape(slot_total, BL, BL)
    right_root_flat = right_roots.reshape(slot_total, BL, BL)

    def one_block(index):
        gradient = blocks_all[index]
        where_slot = slot_of[index]
        left_gram = jnp.dot(gradient, gradient.T, preferred_element_type=jnp.float32)
        right_gram = jnp.dot(gradient.T, gradient, preferred_element_type=jnp.float32)
        applied = jnp.dot(left_root_flat[where_slot], gradient, preferred_element_type=jnp.float32).astype(jnp.bfloat16)
        precond = jnp.dot(applied, right_root_flat[where_slot], preferred_element_type=jnp.float32)
        grad_sq = jnp.sum(jnp.square(gradient.astype(jnp.float32)))
        prec_sq = jnp.sum(jnp.square(precond))
        grafted = (precond * (jnp.sqrt(grad_sq) * lax.rsqrt(prec_sq + epsilon))).astype(jnp.bfloat16)
        return (left_gram, right_gram, grafted)
    left_grams, right_grams, grafted_all = lax.map(one_block, jnp.arange(NB, dtype=jnp.int32))
    new_left = (decay_rate * left_flat).at[slot_of].add((1.0 - decay_rate) * left_grams)
    new_right = (decay_rate * right_flat).at[slot_of].add((1.0 - decay_rate) * right_grams)
    update = grafted_all.reshape(NRB, NCB, BL, BL).transpose(2, 0, 1, 3).reshape(BL, NRB, C)
    return (new_left.reshape(N_DP, MOST, BL, BL), new_right.reshape(N_DP, MOST, BL, BL), update)
```

```python
import functools

import jax
import jax.numpy as jnp
from jax import lax
from jax.experimental import pallas as pl
from jax.experimental.pallas import tpu as pltpu
from jax.sharding import PartitionSpec as P

decay_rate = 0.99
epsilon = 1e-06

NY, NZ = 4, 8
NX = 4
N_DP = NY * NZ
N_T = NX * 2
BL = 1024
ROWS = 128
NRB, NCB = 4, 10
NB = NRB * NCB
TOK = 128
CW = BL // N_DP
GROWS = NCB * CW
GX = GROWS // NX
SPAN = 3
TA = 80
TAH = 48
TB = TOK - TA
TBH = 32
HALF = N_DP // 2

MESH = pl.DeviceIdType.MESH


def remote(src, dst, send_sem, recv_sem, device):
    return pltpu.make_async_remote_copy(
        src_ref=src,
        dst_ref=dst,
        send_sem=send_sem,
        recv_sem=recv_sem,
        device_id=device,
        device_id_type=MESH,
    )


def await_bytes(ref, sem):
    pltpu.make_async_copy(ref, ref, sem).wait()


def kernel(
    x_hbm,
    g_hbm,
    ls_hbm,
    rs_hbm,
    lr_hbm,
    rr_hbm,
    send_idx,
    slot_of,
    nl_hbm,
    nr_hbm,
    up_hbm,
    xall,
    gin,
    gsend,
    gt,
    acc,
    tiles,
    sbuf,
    bt,
    lhs,
    rr,
    ls,
    rs,
    norms,
    pbuf,
    rv,
    up,
    load_sem,
    out_sem,
    xs_sem,
    az_sem,
    ay_sem,
    by_sem,
    bz_sem,
    gs_sem,
    gr_sem,
    gx_sem,
    gc_sem,
    ss_sem,
    sr_sem,
    bx_sem,
    bc_sem,
    nsend_sem,
    nr_sem,
    ps_sem,
    pr_sem,
):
    g = lax.axis_index("dp")
    t = lax.axis_index("tensor")
    y, z = g // NZ, g % NZ
    x, core = t // 2, t % 2
    yp, ym = (y + 1) % NY, (y + NY - 1) % NY
    zp, zm = (z + 1) % NZ, (z + NZ - 1) % NZ
    xp, xm = (x + 1) % NX, (x + NX - 1) % NX
    dev_yp, dev_ym = (yp * NZ + z, t), (ym * NZ + z, t)
    dev_zp, dev_zm = (y * NZ + zp, t), (y * NZ + zm, t)
    dev_xp, dev_xm = (g, xp * 2 + core), (g, xm * 2 + core)
    dev_c = (g, x * 2 + 1 - core)
    lane_t = pl.multiple_of(t * ROWS, ROWS)

    own_x = pltpu.make_async_copy(x_hbm, xall.at[y, z], load_sem.at[0])
    own_x.start()
    j0 = (5 * x) // 2
    load_g = pltpu.make_async_copy(
        g_hbm.at[:, pl.ds(pl.multiple_of(j0 * BL, BL), SPAN * BL)], gin, load_sem.at[1]
    )
    load_g.start()
    later = [
        pltpu.make_async_copy(lr_hbm, lhs.at[:, pl.ds(ROWS, ROWS)], load_sem.at[2]),
        pltpu.make_async_copy(rr_hbm, rr, load_sem.at[3]),
        pltpu.make_async_copy(ls_hbm, ls, load_sem.at[4]),
        pltpu.make_async_copy(rs_hbm, rs, load_sem.at[5]),
    ]
    for copy in later:
        copy.start()

    barrier = pltpu.get_barrier_semaphore()

    def greet_dp(d, carry):
        pl.semaphore_signal(barrier, inc=1, device_id=((g + d) % N_DP, t), device_id_type=MESH)
        return carry

    def greet_tensor(d, carry):
        pl.semaphore_signal(barrier, inc=1, device_id=(g, (t + d) % N_T), device_id_type=MESH)
        return carry

    lax.fori_loop(1, N_DP, greet_dp, 0)
    lax.fori_loop(1, N_T, greet_tensor, 0)
    pl.semaphore_wait(barrier, N_DP + N_T - 2)

    def az(k, right):
        zs = (z + NZ - k) % NZ if right else (z + k) % NZ
        if k < 3:
            rows = pl.ds(0, TA)
        else:
            rows = pl.ds(0, TAH) if right else pl.ds(TAH, TA - TAH)
        ref = xall.at[y, zs, rows]
        n = k * 2 + (0 if right else 1)
        return remote(ref, ref, xs_sem.at[n], az_sem.at[n], dev_zp if right else dev_zm)

    def by(k, right):
        if k == 0:
            ys, rows = y, pl.ds(TA, TB)
        elif right:
            ys, rows = ym, pl.ds(TA, TBH)
        else:
            ys, rows = yp, pl.ds(TA + TBH, TB - TBH)
        ref = xall.at[ys, z, rows]
        n = k * 2 + (0 if right else 1)
        return remote(ref, ref, xs_sem.at[8 + n], by_sem.at[n], dev_yp if right else dev_ym)

    def bz(k, right):
        zs = (z + NZ - k) % NZ if right else (z + k) % NZ
        if k < 3:
            rows = pl.ds(TA, TB)
        else:
            rows = pl.ds(TA, TBH) if right else pl.ds(TA + TBH, TB - TBH)
        ref = xall.at[:, zs, rows]
        n = k * 2 + (0 if right else 1)
        return remote(ref, ref, xs_sem.at[12 + n], bz_sem.at[n], dev_zp if right else dev_zm)

    def ay(k, right):
        if k == 0:
            ys, zs = y, pl.ds(0, NZ)
        elif right:
            ys, zs = ym, pl.ds(0, NZ // 2)
        else:
            ys, zs = yp, pl.ds(NZ // 2, NZ // 2)
        ref = xall.at[ys, zs, pl.ds(0, TA)]
        n = k * 2 + (0 if right else 1)
        return remote(ref, ref, xs_sem.at[20 + n], ay_sem.at[n], dev_yp if right else dev_ym)

    own_x.wait()
    for right in (True, False):
        az(0, right).start()
        by(0, right).start()

    load_g.wait()
    offset = pl.multiple_of(((5 * x) % 2) * 16, 16)
    gx_rows = pl.ds(pl.multiple_of(x * GX, 16), GX)
    sends_g = core == y // 2

    @pl.when(sends_g)
    def _():
        for j in range(SPAN):
            block = gin[:, j * BL : (j + 1) * BL].T
            gsend[:, j * CW : (j + 1) * CW, :] = block.reshape(N_DP, CW, TOK)

        lanes = pl.ds(pl.multiple_of(g * TOK, TOK), TOK)
        own = pltpu.make_async_copy(
            gsend.at[g, pl.ds(offset, GX)], gt.at[gx_rows, lanes], gr_sem
        )
        own.start()

        def send_g(d, carry):
            to = (g + d) % N_DP
            remote(
                gsend.at[to, pl.ds(offset, GX)], gt.at[gx_rows, lanes], gs_sem, gr_sem, (to, t)
            ).start()
            return carry

        lax.fori_loop(1, N_DP, send_g, 0)

    for k in range(1, 4):
        for right in (True, False):
            az(k - 1, right).wait_recv()
            az(k, right).start()
        if k == 1:
            for right in (True, False):
                by(0, right).wait_recv()
                by(1, right).start()
    for right in (True, False):
        by(1, right).wait_recv()
    for right in (True, False):
        bz(0, right).start()
    for right in (True, False):
        az(3, right).wait_recv()
    for right in (True, False):
        ay(0, right).start()

    half_lanes = pl.ds(pl.multiple_of(core * HALF * TOK, HALF * TOK), HALF * TOK)
    await_bytes(gt.at[gx_rows, half_lanes], gr_sem)

    def gxc(k, right):
        if k == 0:
            start, size = x * GX, GX
        elif right:
            start, size = xm * GX, 48
        else:
            start, size = xp * GX + 48, 32
        ref = gt.at[pl.ds(pl.multiple_of(start, 16), size), half_lanes]
        n = k * 2 + (0 if right else 1)
        return remote(ref, ref, xs_sem.at[24 + n], gx_sem.at[n], dev_xp if right else dev_xm)

    for right in (True, False):
        gxc(0, right).start()
    for right in (True, False):
        bz(0, right).wait_recv()
        bz(1, right).start()
    for right in (True, False):
        gxc(0, right).wait_recv()
        gxc(1, right).start()
    for right in (True, False):
        bz(1, right).wait_recv()
        bz(2, right).start()
    for right in (True, False):
        ay(0, right).wait_recv()
        ay(1, right).start()
    for right in (True, False):
        gxc(1, right).wait_recv()
    gcc = remote(
        gt.at[:, half_lanes], gt.at[:, half_lanes], xs_sem.at[28], gc_sem, dev_c
    )
    gcc.start()
    for right in (True, False):
        bz(2, right).wait_recv()
        bz(3, right).start()
    gcc.wait_recv()
    for right in (True, False):
        ay(1, right).wait_recv()
    for right in (True, False):
        bz(3, right).wait_recv()

    acc[...] = jnp.zeros_like(acc)
    depth = 4 * TOK

    def add_tokens(n, carry):
        lanes = pl.ds(pl.multiple_of(n * depth, depth), depth)
        part = xall[n // 2, pl.ds((n % 2) * 4, 4)].reshape(depth, NRB * ROWS)
        acc[...] += jnp.dot(gt[:, lanes], part, preferred_element_type=jnp.float32)
        return carry

    lax.fori_loop(0, N_DP * TOK // depth, add_tokens, 0)
    for i in range(NRB):
        for j in range(NCB):
            tiles[i * NCB + j] = acc[
                j * CW : (j + 1) * CW, i * ROWS : (i + 1) * ROWS
            ].astype(jnp.bfloat16)
    tiles[NB] = jnp.zeros((CW, ROWS), jnp.bfloat16)

    bt_rows = pl.ds(pl.multiple_of(g * CW, CW), CW)
    bt_lanes = pl.ds(lane_t, ROWS)
    for s in range(2):

        def send_block(d, carry):
            to = (g + d) % N_DP
            sbuf[s, to] = tiles[send_idx[to * 2 + s]]
            remote(
                sbuf.at[s, to], bt.at[s, bt_rows, bt_lanes], ss_sem.at[s], sr_sem.at[s], (to, t)
            ).start()
            return carry

        sbuf[s, g] = tiles[send_idx[g * 2 + s]]
        pltpu.make_async_copy(sbuf.at[s, g], bt.at[s, bt_rows, bt_lanes], sr_sem.at[s]).start()
        lax.fori_loop(1, N_DP, send_block, 0)

    def lanes_of(xs, cs):
        return pl.ds(pl.multiple_of((xs * 2 + cs) * ROWS, ROWS), ROWS)

    def bxc(s, k, right):
        if k == 0:
            xs, rows = x, pl.ds(0, BL)
        elif right:
            xs, rows = xm, pl.ds(0, BL // 2)
        else:
            xs, rows = xp, pl.ds(BL // 2, BL // 2)
        ref = bt.at[s, rows, lanes_of(xs, core)]
        n = s * 4 + k * 2 + (0 if right else 1)
        return remote(ref, ref, xs_sem.at[29 + n], bx_sem.at[n], dev_xp if right else dev_xm)

    def bcc(s, step, sending=True):
        xs = (x + NX - step) % NX
        ref = bt.at[s, :, lanes_of(xs, core if sending else 1 - core)]
        n = s * 4 + step
        return remote(ref, ref, xs_sem.at[37 + n], bc_sem.at[n], dev_c)

    def gather_start(s):
        await_bytes(bt.at[s, :, bt_lanes], sr_sem.at[s])
        for right in (True, False):
            bxc(s, 0, right).start()
        bcc(s, 0).start()

    def gather_middle(s):
        bxc(s, 0, True).wait_recv()
        bxc(s, 1, True).start()
        bcc(s, 1).start()
        bxc(s, 0, False).wait_recv()
        bxc(s, 1, False).start()
        bcc(s, 3).start()

    def gather_end(s):
        for right in (True, False):
            bxc(s, 1, right).wait_recv()
        bcc(s, 2).start()
        for step in (0, 1, 3, 2):
            bcc(s, step, False).wait_recv()

    def norm_copy(s, d):
        ref = norms.at[s, t]
        return remote(ref, ref, nsend_sem.at[s], nr_sem.at[s, d], (g, (t + d) % N_T))

    def precondition(s):
        lhs[s, 0:ROWS] = bt[s, pl.ds(lane_t, ROWS), :]
        both = lax.dot_general(
            lhs[s], bt[s], (((1,), (1,)), ((), ())), preferred_element_type=jnp.float32
        )
        rs[s] = decay_rate * rs[s] + (1.0 - decay_rate) * both[0:ROWS]
        pltpu.make_async_copy(rs.at[s], nr_hbm.at[s], out_sem.at[s]).start()
        applied = both[ROWS:].astype(jnp.bfloat16)
        precond = jnp.dot(applied, rr[s], preferred_element_type=jnp.float32)
        own = bt[s, :, bt_lanes].astype(jnp.float32)
        norms[s, t, 0:8] = jnp.sum((own * own).reshape(-1, 8, ROWS), axis=0)
        squares = precond * precond
        folded = jnp.sum(squares.reshape(-1, 8, BL), axis=0)
        total = folded[:, 0:ROWS]
        for m in range(1, BL // ROWS):
            total = total + folded[:, m * ROWS : (m + 1) * ROWS]
        norms[s, t, 8:16] = total
        for d in range(1, N_T):
            norm_copy(s, d).start()
        for d in range(1, N_T):
            norm_copy(s, d).wait_recv()
        sums = jnp.sum(norms[s], axis=0)
        grad_sq = jnp.sum(sums[0:8], keepdims=True)
        prec_sq = jnp.sum(sums[8:16], keepdims=True)
        scale = jnp.sqrt(grad_sq) * lax.rsqrt(prec_sq + epsilon)
        grafted = precond * scale
        pbuf[s] = grafted.reshape(ROWS, 8, ROWS).reshape(N_DP, 32, ROWS).astype(jnp.bfloat16)
        pltpu.make_async_copy(pbuf.at[s, g], rv.at[s, g], pr_sem.at[s]).start()

        def send_back(d, carry):
            to = (g + d) % N_DP
            remote(pbuf.at[s, to], rv.at[s, g], ps_sem.at[s], pr_sem.at[s], (to, t)).start()
            return carry

        lax.fori_loop(1, N_DP, send_back, 0)

    def left(s):
        own = bt[s, :, bt_lanes]
        gram = lax.dot_general(
            own, bt[s], (((0,), (0,)), ((), ())), preferred_element_type=jnp.float32
        )
        ls[s] = decay_rate * ls[s] + (1.0 - decay_rate) * gram
        pltpu.make_async_copy(ls.at[s], nl_hbm.at[s], out_sem.at[2 + s]).start()

    gather_start(0)
    gather_start(1)
    gather_middle(0)
    for copy in later:
        copy.wait()
    gather_end(0)
    gather_middle(1)
    precondition(0)
    gather_end(1)
    precondition(1)
    left(0)
    left(1)

    for s in range(2):
        await_bytes(rv.at[s], pr_sem.at[s])

    def place(b, carry):
        slot = slot_of[b]
        up[b] = rv[slot % 2, slot // 2]
        return carry

    lax.fori_loop(0, NB, place, 0)
    write = pltpu.make_async_copy(up, up_hbm, out_sem.at[4])
    write.start()

    for k in range(4):
        for right in (True, False):
            az(k, right).wait_send()
            bz(k, right).wait_send()
    for k in range(2):
        for right in (True, False):
            by(k, right).wait_send()
            ay(k, right).wait_send()
            gxc(k, right).wait_send()
    gcc.wait_send()

    @pl.when(sends_g)
    def _():
        await_bytes(gsend.at[pl.ds(0, N_DP - 1), pl.ds(0, GX)], gs_sem)

    for s in range(2):
        await_bytes(sbuf.at[s, pl.ds(0, N_DP - 1)], ss_sem.at[s])
        for k in range(2):
            for right in (True, False):
                bxc(s, k, right).wait_send()
        for step in range(4):
            bcc(s, step).wait_send()
        await_bytes(norms.at[s, pl.ds(0, N_T - 1)], nsend_sem.at[s])
        await_bytes(pbuf.at[s, pl.ds(0, N_DP - 1)], ps_sem.at[s])
        pltpu.make_async_copy(rs.at[s], nr_hbm.at[s], out_sem.at[s]).wait()
        pltpu.make_async_copy(ls.at[s], nl_hbm.at[s], out_sem.at[2 + s]).wait()
    write.wait()


def body(
    layer_inputs,
    output_grads,
    left_stats,
    right_stats,
    left_roots,
    right_roots,
    owner_blocks,
    block_counts,
):
    f32, bf16 = jnp.float32, jnp.bfloat16
    live = jnp.arange(2, dtype=jnp.int32)[None, :] < block_counts[:, None]
    listed = jnp.where(live, jnp.clip(owner_blocks, 0, NB - 1), NB).reshape(-1)
    matches = listed[None, :] == jnp.arange(NB, dtype=jnp.int32)[:, None]
    slot_of = jnp.sum(
        jnp.where(matches, jnp.arange(2 * N_DP, dtype=jnp.int32)[None, :], 0), axis=1
    )
    dma = pltpu.SemaphoreType.DMA
    hbm = pl.BlockSpec(memory_space=pl.ANY)
    smem = pl.BlockSpec(memory_space=pltpu.SMEM)
    new_left, new_right, update = pl.pallas_call(
        kernel,
        out_shape=(
            jax.ShapeDtypeStruct((2, ROWS, BL), f32),
            jax.ShapeDtypeStruct((2, ROWS, BL), f32),
            jax.ShapeDtypeStruct((NB, 32, ROWS), bf16),
        ),
        in_specs=[hbm] * 6 + [smem] * 2,
        out_specs=(hbm, hbm, hbm),
        scratch_shapes=[
            pltpu.VMEM((NY, NZ, TOK, NRB * ROWS), bf16),
            pltpu.VMEM((TOK, SPAN * BL), bf16),
            pltpu.VMEM((N_DP, SPAN * CW, TOK), bf16),
            pltpu.VMEM((GROWS, N_DP * TOK), bf16),
            pltpu.VMEM((GROWS, NRB * ROWS), f32),
            pltpu.VMEM((NB + 1, CW, ROWS), bf16),
            pltpu.VMEM((2, N_DP, CW, ROWS), bf16),
            pltpu.VMEM((2, BL, BL), bf16),
            pltpu.VMEM((2, 2 * ROWS, BL), bf16),
            pltpu.VMEM((2, BL, BL), bf16),
            pltpu.VMEM((2, ROWS, BL), f32),
            pltpu.VMEM((2, ROWS, BL), f32),
            pltpu.VMEM((2, N_T, 16, ROWS), f32),
            pltpu.VMEM((2, N_DP, 32, ROWS), bf16),
            pltpu.VMEM((2, N_DP, 32, ROWS), bf16),
            pltpu.VMEM((NB, 32, ROWS), bf16),
            dma((6,)),
            dma((5,)),
            dma((45,)),
            dma((8,)),
            dma((4,)),
            dma((4,)),
            dma((8,)),
            dma,
            dma,
            dma((4,)),
            dma,
            dma((2,)),
            dma((2,)),
            dma((8,)),
            dma((8,)),
            dma((2,)),
            dma((2, N_T)),
            dma((2,)),
            dma((2,)),
        ],
        compiler_params=pltpu.CompilerParams(
            collective_id=0, has_side_effects=True, vmem_limit_bytes=48 * 1024 * 1024
        ),
        cost_estimate=pl.CostEstimate(
            flops=4_000_000_000, bytes_accessed=16_000_000, transcendentals=0
        ),
    )(
        layer_inputs.reshape(TOK, NRB * ROWS),
        output_grads,
        left_stats[0],
        right_stats[0],
        left_roots[0],
        right_roots[0],
        listed,
        slot_of,
    )
    update = update.reshape(NB, 4, BL).transpose(1, 0, 2).reshape(4, NRB, NCB * BL)
    return (new_left[None], new_right[None], update)


def solution(mesh):
    placed = (
        P("dp", None, "tensor"),
        P("dp", None),
        P("dp", None, "tensor", None),
        P("dp", None, "tensor", None),
        P("dp", None, "tensor", None),
        P("dp", None, None, None),
        P(),
        P(),
    )
    return jax.shard_map(
        body,
        mesh=mesh,
        in_specs=placed,
        out_specs=(
            P("dp", None, "tensor", None),
            P("dp", None, "tensor", None),
            P(("tensor", "dp"), None, None),
        ),
        check_vma=False,
    )
```

```python
import functools

import jax
import jax.numpy as jnp
from jax import lax
from jax.experimental import pallas as pl
from jax.experimental.pallas import tpu as pltpu
from jax.sharding import PartitionSpec as P

decay_rate = 0.99
epsilon = 1e-06

NY, NZ = 4, 8
NX = 4
N_DP = NY * NZ
N_T = NX * 2
BL = 1024
ROWS = 128
NRB, NCB = 4, 10
NB = NRB * NCB
TOK = 128
CW = BL // N_DP
GROWS = NCB * CW
GX = GROWS // NX
SPAN = 3
TA = 80
TAH = 48
TB = TOK - TA
TBH = 32
HALF = N_DP // 2

MESH = pl.DeviceIdType.MESH


def remote(src, dst, send_sem, recv_sem, device):
    return pltpu.make_async_remote_copy(
        src_ref=src,
        dst_ref=dst,
        send_sem=send_sem,
        recv_sem=recv_sem,
        device_id=device,
        device_id_type=MESH,
    )


def await_bytes(ref, sem):
    pltpu.make_async_copy(ref, ref, sem).wait()


def kernel(
    x_hbm,
    g_hbm,
    lr_hbm,
    rr_hbm,
    send_idx,
    slot_of,
    nl_out,
    nr_out,
    up_out,
    xall,
    gin,
    gsend,
    gt,
    acc,
    tiles,
    sbuf,
    bt,
    lhs,
    rr,
    pre,
    norms,
    pbuf,
    rv,
    load_sem,
    greet_sem,
    sent,
    az_sem,
    ay_sem,
    ay2_sem,
    by_sem,
    bz_sem,
    gs_sem,
    gr_sem,
    gx_sem,
    gc_sem,
    ss_sem,
    sr_sem,
    bx_sem,
    bc_sem,
    nsend_sem,
    nr_sem,
    ps_sem,
    pr_sem,
):
    g = lax.axis_index("dp")
    t = lax.axis_index("tensor")
    y, z = g // NZ, g % NZ
    x, core = t // 2, t % 2
    yp, ym = (y + 1) % NY, (y + NY - 1) % NY
    zp, zm = (z + 1) % NZ, (z + NZ - 1) % NZ
    xp, xm = (x + 1) % NX, (x + NX - 1) % NX
    dev_yp, dev_ym = (yp * NZ + z, t), (ym * NZ + z, t)
    dev_zp, dev_zm = (y * NZ + zp, t), (y * NZ + zm, t)
    dev_xp, dev_xm = (g, xp * 2 + core), (g, xm * 2 + core)
    dev_c = (g, x * 2 + 1 - core)
    lane_t = pl.multiple_of(t * ROWS, ROWS)
    both_ways = (True, False)

    barrier = pltpu.get_barrier_semaphore()
    z_line = [(y * NZ + (z + k) % NZ, t) for k in range(1, NZ)]
    y_line = [((y + k) % NY * NZ + z, t) for k in range(1, NY)]
    near = z_line + y_line + [dev_xp, dev_xm, dev_c]
    for device in near:
        pl.semaphore_signal(barrier, inc=1, device_id=device, device_id_type=MESH)

    j0 = (5 * x) // 2
    load_g = pltpu.make_async_copy(
        g_hbm.at[:, pl.ds(pl.multiple_of(j0 * BL, BL), SPAN * BL)], gin, load_sem.at[1]
    )
    load_g.start()
    own_x = pltpu.make_async_copy(x_hbm, xall.at[y, z], load_sem.at[0])
    own_x.start()
    later = [
        pltpu.make_async_copy(lr_hbm, lhs.at[:, pl.ds(ROWS, ROWS)], load_sem.at[2]),
        pltpu.make_async_copy(rr_hbm, rr, load_sem.at[3]),
    ]
    load_g.wait()
    sends_g = core == y // 2

    @pl.when(sends_g)
    def _():
        for j in range(SPAN):
            block = gin[:, j * BL : (j + 1) * BL].T
            gsend[:, j * CW : (j + 1) * CW, :] = block.reshape(N_DP, CW, TOK)

    own_x.wait()
    pl.semaphore_wait(barrier, len(near))

    z_off = (0, NZ - 1, 1, NZ - 2, 2, NZ - 3, 3, 4)

    def az(k, right):
        zs = (z + NZ - k) % NZ if right else (z + k) % NZ
        if k < 3:
            rows = pl.ds(0, TA)
        else:
            rows = pl.ds(0, TAH) if right else pl.ds(TAH, TA - TAH)
        ref = xall.at[y, zs, rows]
        n = k * 2 + (0 if right else 1)
        return remote(ref, ref, sent.at[n], az_sem.at[n], dev_zp if right else dev_zm)

    def ay(p, right):
        ref = xall.at[y, (z + z_off[p]) % NZ, pl.ds(0, TA)]
        n = p * 2 + (0 if right else 1)
        return remote(ref, ref, sent.at[8 + n], ay_sem.at[n], dev_yp if right else dev_ym)

    def ay2(p):
        right = p % 2 == 0
        ref = xall.at[ym if right else yp, (z + z_off[p]) % NZ, pl.ds(0, TA)]
        return remote(ref, ref, sent.at[24 + p], ay2_sem.at[p], dev_yp if right else dev_ym)

    def by(k, right):
        if k == 0:
            ys, rows = y, pl.ds(TA, TB)
        elif right:
            ys, rows = ym, pl.ds(TA, TBH)
        else:
            ys, rows = yp, pl.ds(TA + TBH, TB - TBH)
        ref = xall.at[ys, z, rows]
        n = k * 2 + (0 if right else 1)
        return remote(ref, ref, sent.at[32 + n], by_sem.at[n], dev_yp if right else dev_ym)

    def bz(q, k, right):
        ys = (y, ym, yp, (y + 2) % NY)[q]
        zs = (z + NZ - k) % NZ if right else (z + k) % NZ
        if k < 3:
            rows = pl.ds(TA, TB)
        else:
            rows = pl.ds(TA, TBH) if right else pl.ds(TA + TBH, TB - TBH)
        ref = xall.at[ys, zs, rows]
        n = q * 8 + k * 2 + (0 if right else 1)
        return remote(ref, ref, sent.at[36 + n], bz_sem.at[n], dev_zp if right else dev_zm)

    def az_step(k):
        for right in both_ways:
            az(k - 1, right).wait_recv()
            az(k, right).start()
            p = 2 * k - 1 if right else 2 * k
            for way in both_ways:
                ay(p, way).start()

    def bz_step(q, k):
        for right in both_ways:
            if k:
                bz(q, k - 1, right).wait_recv()
            bz(q, k, right).start()

    def ay2_step(p):
        ay(p, p % 2 == 0).wait_recv()
        ay2(p).start()

    for right in both_ways:
        az(0, right).start()
    for right in both_ways:
        by(0, right).start()

    for device in y_line:
        pl.semaphore_signal(greet_sem, inc=1, device_id=device, device_id_type=MESH)

    offset = pl.multiple_of(((5 * x) % 2) * 16, 16)
    gx_rows = pl.ds(pl.multiple_of(x * GX, 16), GX)
    own_lanes = pl.ds(pl.multiple_of(g * TOK, TOK), TOK)

    def send_g(to):
        remote(
            gsend.at[to, pl.ds(offset, GX)], gt.at[gx_rows, own_lanes], gs_sem, gr_sem, (to, t)
        ).start()

    @pl.when(sends_g)
    def _():
        pltpu.make_async_copy(
            gsend.at[g, pl.ds(offset, GX)], gt.at[gx_rows, own_lanes], gr_sem
        ).start()
        for k in range(1, NZ):
            send_g(y * NZ + (z + k) % NZ)

    for right in both_ways:
        ay(0, right).start()
    pl.semaphore_wait(greet_sem, len(y_line))

    @pl.when(sends_g)
    def _():
        def send_rest(d, carry):
            send_g((y * NZ + d) % N_DP)
            return carry

        lax.fori_loop(NZ, N_DP, send_rest, 0)

    half_lanes = pl.ds(pl.multiple_of(core * HALF * TOK, HALF * TOK), HALF * TOK)
    other_lanes = pl.ds(pl.multiple_of((1 - core) * HALF * TOK, HALF * TOK), HALF * TOK)

    quarter = HALF * TOK // 2

    def gxc(k, right):
        xs = x if k < 2 else (xm if right else xp)
        first = right if k != 1 else not right
        rows = pl.ds(pl.multiple_of(xs * GX, 16), GX)
        start = core * HALF * TOK + (0 if first else quarter)
        ref = gt.at[rows, pl.ds(pl.multiple_of(start, quarter), quarter)]
        n = k * 2 + (0 if right else 1)
        return remote(ref, ref, sent.at[68 + n], gx_sem.at[n], dev_xp if right else dev_xm)

    def gcc(step):
        rows = pl.ds(pl.multiple_of((x + NX - step) % NX * GX, 16), GX)
        ref = gt.at[rows, half_lanes]
        return remote(ref, ref, sent.at[74 + step], gc_sem.at[step], dev_c)

    def step_by():
        for right in both_ways:
            by(0, right).wait_recv()
        for right in both_ways:
            by(1, right).start()

    def step_by1():
        for right in both_ways:
            by(1, right).wait_recv()

    def step_G0():
        await_bytes(gt.at[gx_rows, half_lanes], gr_sem)
        for k in range(2):
            for right in both_ways:
                gxc(k, right).start()
        gcc(0).start()

    def step_G1():
        for right in both_ways:
            gxc(0, right).wait_recv()
            gxc(2, right).start()
        for right in both_ways:
            gxc(1, right).wait_recv()
            gcc(1 if right else 3).start()

    def step_G2():
        for right in both_ways:
            gxc(2, right).wait_recv()
        gcc(2).start()

    def step_ay7():
        for right in both_ways:
            az(3, right).wait_recv()
        for right in both_ways:
            ay(7, right).start()

    def step_L():
        for copy in later:
            copy.start()

    def step_GE():
        for step in (0, 1, 3, 2):
            gcc(step).wait_recv()

    def step_XE():
        for p in range(NZ):
            ay(p, p % 2 == 1).wait_recv()
        for q in range(NY):
            for right in both_ways:
                bz(q, 3, right).wait_recv()
        for p in range(NZ):
            ay2(p).wait_recv()

    bz_step(0, 0)
    az_step(1)
    step_by()
    bz_step(1, 0)
    bz_step(2, 0)
    bz_step(0, 1)
    az_step(2)
    ay2_step(0)
    step_G0()
    step_by1()
    bz_step(3, 0)
    bz_step(1, 1)
    bz_step(2, 1)
    step_L()
    bz_step(0, 2)
    step_G1()
    az_step(3)
    ay2_step(1)
    ay2_step(2)
    bz_step(3, 1)
    bz_step(1, 2)
    bz_step(2, 2)
    step_G2()
    bz_step(0, 3)
    step_ay7()
    ay2_step(3)
    ay2_step(4)
    bz_step(3, 2)
    bz_step(1, 3)
    bz_step(2, 3)
    ay2_step(5)
    ay2_step(6)
    bz_step(3, 3)
    ay2_step(7)
    step_XE()
    step_GE()

    acc[...] = jnp.zeros_like(acc)
    depth = 4 * TOK

    def add_tokens(n, carry):
        lanes = pl.ds(pl.multiple_of(n * depth, depth), depth)
        part = xall[n // 2, pl.ds((n % 2) * 4, 4)].reshape(depth, NRB * ROWS)
        acc[...] += jnp.dot(gt[:, lanes], part, preferred_element_type=jnp.float32)
        return carry

    lax.fori_loop(0, N_DP * TOK // depth, add_tokens, 0)
    for i in range(NRB):
        for j in range(NCB):
            tiles[i * NCB + j] = acc[
                j * CW : (j + 1) * CW, i * ROWS : (i + 1) * ROWS
            ].astype(jnp.bfloat16)
    tiles[NB] = jnp.zeros((CW, ROWS), jnp.bfloat16)

    bt_rows = pl.ds(pl.multiple_of(g * CW, CW), CW)
    bt_lanes = pl.ds(lane_t, ROWS)
    def send_blocks(s):
        def send_block(d, carry):
            to = (g + d) % N_DP
            sbuf[s, to] = tiles[send_idx[to * 2 + s]]
            remote(
                sbuf.at[s, to], bt.at[s, bt_rows, bt_lanes], ss_sem.at[s], sr_sem.at[s], (to, t)
            ).start()
            return carry

        sbuf[s, g] = tiles[send_idx[g * 2 + s]]
        pltpu.make_async_copy(sbuf.at[s, g], bt.at[s, bt_rows, bt_lanes], sr_sem.at[s]).start()
        lax.fori_loop(1, N_DP, send_block, 0)

    def lanes_of(xs, cs):
        return pl.ds(pl.multiple_of((xs * 2 + cs) * ROWS, ROWS), ROWS)

    def bxc(s, k, right):
        xs = x if k < 2 else (xm if right else xp)
        first = right if k != 1 else not right
        rows = pl.ds(0 if first else BL // 2, BL // 2)
        ref = bt.at[s, rows, lanes_of(xs, core)]
        n = s * 6 + k * 2 + (0 if right else 1)
        return remote(ref, ref, sent.at[78 + n], bx_sem.at[n], dev_xp if right else dev_xm)

    def bcc(s, step):
        ref = bt.at[s, :, lanes_of((x + NX - step) % NX, core)]
        n = s * 4 + step
        return remote(ref, ref, sent.at[90 + n], bc_sem.at[n], dev_c)

    def gather_start(s):
        await_bytes(bt.at[s, :, bt_lanes], sr_sem.at[s])
        for k in range(2):
            for right in both_ways:
                bxc(s, k, right).start()
        bcc(s, 0).start()

    def gather_middle(s):
        for right in both_ways:
            bxc(s, 0, right).wait_recv()
            bxc(s, 2, right).start()
        for right in both_ways:
            bxc(s, 1, right).wait_recv()
            bcc(s, 1 if right else 3).start()

    def gather_end(s):
        for right in both_ways:
            bxc(s, 2, right).wait_recv()
        bcc(s, 2).start()
        for step in (0, 1, 3, 2):
            bcc(s, step).wait_recv()

    def norm_copy(s, d):
        ref = norms.at[s, t]
        return remote(ref, ref, nsend_sem.at[s], nr_sem.at[s, d], (g, (t + d) % N_T))

    def precondition(s):
        lhs[s, 0:ROWS] = bt[s, pl.ds(lane_t, ROWS), :]
        both = lax.dot_general(
            lhs[s], bt[s], (((1,), (1,)), ((), ())), preferred_element_type=jnp.float32
        )
        nr_out[s] = both[0:ROWS]
        applied = both[ROWS:].astype(jnp.bfloat16)
        precond = jnp.dot(applied, rr[s], preferred_element_type=jnp.float32)
        pre[s] = precond
        own = bt[s, :, bt_lanes].astype(jnp.float32)
        norms[s, t, 0:8] = jnp.sum((own * own).reshape(-1, 8, ROWS), axis=0)
        squares = precond * precond
        folded = jnp.sum(squares.reshape(-1, 8, BL), axis=0)
        total = folded[:, 0:ROWS]
        for m in range(1, BL // ROWS):
            total = total + folded[:, m * ROWS : (m + 1) * ROWS]
        norms[s, t, 8:16] = total
        for d in range(1, N_T):
            norm_copy(s, d).start()

    def send_rows(s):
        for d in range(1, N_T):
            norm_copy(s, d).wait_recv()
        sums = jnp.sum(norms[s], axis=0)
        grad_sq = jnp.sum(sums[0:8], keepdims=True)
        prec_sq = jnp.sum(sums[8:16], keepdims=True)
        scale = jnp.sqrt(grad_sq) * lax.rsqrt(prec_sq + epsilon)
        grafted = pre[s] * scale
        pbuf[s] = grafted.reshape(ROWS, 8, ROWS).reshape(N_DP, 32, ROWS).astype(jnp.bfloat16)
        pltpu.make_async_copy(pbuf.at[s, g], rv.at[s, g], pr_sem.at[s]).start()

        def send_back(d, carry):
            to = (g + d) % N_DP
            remote(pbuf.at[s, to], rv.at[s, g], ps_sem.at[s], pr_sem.at[s], (to, t)).start()
            return carry

        lax.fori_loop(1, N_DP, send_back, 0)

    def left(s):
        own = bt[s, :, bt_lanes]
        nl_out[s] = lax.dot_general(
            own, bt[s], (((0,), (0,)), ((), ())), preferred_element_type=jnp.float32
        )

    send_blocks(0)
    gather_start(0)
    send_blocks(1)
    gather_middle(0)
    gather_start(1)
    for copy in later:
        copy.wait()
    gather_end(0)
    precondition(0)
    gather_middle(1)
    left(0)
    send_rows(0)
    gather_end(1)
    precondition(1)
    left(1)
    send_rows(1)

    for k in range(4):
        for right in both_ways:
            az(k, right).wait_send()
            for q in range(NY):
                bz(q, k, right).wait_send()
    for p in range(NZ):
        for right in both_ways:
            ay(p, right).wait_send()
        ay2(p).wait_send()
    for right in both_ways:
        for k in range(2):
            by(k, right).wait_send()
        for k in range(3):
            gxc(k, right).wait_send()
    for step in range(4):
        gcc(step).wait_send()

    @pl.when(sends_g)
    def _():
        await_bytes(gsend.at[pl.ds(0, N_DP - 1), pl.ds(0, GX)], gs_sem)

    for s in range(2):
        await_bytes(sbuf.at[s, pl.ds(0, N_DP - 1)], ss_sem.at[s])
        for k in range(3):
            for right in both_ways:
                bxc(s, k, right).wait_send()
        for step in range(4):
            bcc(s, step).wait_send()
        await_bytes(norms.at[s, pl.ds(0, N_T - 1)], nsend_sem.at[s])
        await_bytes(pbuf.at[s, pl.ds(0, N_DP - 1)], ps_sem.at[s])

    for s in range(2):
        await_bytes(rv.at[s], pr_sem.at[s])

    def place(b, carry):
        slot = slot_of[b]
        rows = rv[slot % 2, slot // 2]
        for k in range(4):
            up_out[k, b] = rows[k * 8 : (k + 1) * 8]
        return carry

    lax.fori_loop(0, NB, place, 0)

def body(
    layer_inputs,
    output_grads,
    left_stats,
    right_stats,
    left_roots,
    right_roots,
    owner_blocks,
    block_counts,
):
    f32, bf16 = jnp.float32, jnp.bfloat16
    live = jnp.arange(2, dtype=jnp.int32)[None, :] < block_counts[:, None]
    listed = jnp.where(live, jnp.clip(owner_blocks, 0, NB - 1), NB).reshape(-1)
    matches = listed[None, :] == jnp.arange(NB, dtype=jnp.int32)[:, None]
    slot_of = jnp.sum(
        jnp.where(matches, jnp.arange(2 * N_DP, dtype=jnp.int32)[None, :], 0), axis=1
    )
    dma = pltpu.SemaphoreType.DMA
    hbm = pl.BlockSpec(memory_space=pltpu.HBM)
    vmem = pl.BlockSpec(memory_space=pltpu.VMEM)
    smem = pl.BlockSpec(memory_space=pltpu.SMEM)
    left_gram, right_gram, update = pl.pallas_call(
        kernel,
        out_shape=(
            jax.ShapeDtypeStruct((2, ROWS, BL), f32),
            jax.ShapeDtypeStruct((2, ROWS, BL), f32),
            jax.ShapeDtypeStruct((4, NB, 8, ROWS), bf16),
        ),
        in_specs=[hbm] * 4 + [smem] * 2,
        out_specs=(vmem, vmem, vmem),
        scratch_shapes=[
            pltpu.VMEM((NY, NZ, TOK, NRB * ROWS), bf16),
            pltpu.VMEM((TOK, SPAN * BL), bf16),
            pltpu.VMEM((N_DP, SPAN * CW, TOK), bf16),
            pltpu.VMEM((GROWS, N_DP * TOK), bf16),
            pltpu.VMEM((GROWS, NRB * ROWS), f32),
            pltpu.VMEM((NB + 1, CW, ROWS), bf16),
            pltpu.VMEM((2, N_DP, CW, ROWS), bf16),
            pltpu.VMEM((2, BL, BL), bf16),
            pltpu.VMEM((2, 2 * ROWS, BL), bf16),
            pltpu.VMEM((2, BL, BL), bf16),
            pltpu.VMEM((2, ROWS, BL), f32),
            pltpu.VMEM((2, N_T, 16, ROWS), f32),
            pltpu.VMEM((2, N_DP, 32, ROWS), bf16),
            pltpu.VMEM((2, N_DP, 32, ROWS), bf16),
            dma((4,)),
            pltpu.SemaphoreType.REGULAR,
            dma((98,)),
            dma((8,)),
            dma((16,)),
            dma((8,)),
            dma((4,)),
            dma((32,)),
            dma,
            dma,
            dma((6,)),
            dma((4,)),
            dma((2,)),
            dma((2,)),
            dma((12,)),
            dma((8,)),
            dma((2,)),
            dma((2, N_T)),
            dma((2,)),
            dma((2,)),
        ],
        compiler_params=pltpu.CompilerParams(
            collective_id=0, has_side_effects=True, vmem_limit_bytes=48 * 1024 * 1024
        ),
        cost_estimate=pl.CostEstimate(
            flops=4_000_000_000, bytes_accessed=16_000_000, transcendentals=0
        ),
    )(
        layer_inputs.reshape(TOK, NRB * ROWS),
        output_grads,
        left_roots[0],
        right_roots[0],
        listed,
        slot_of,
    )
    update = update.reshape(4, NRB, NCB * BL)
    new_left = decay_rate * left_stats + (1.0 - decay_rate) * left_gram[None]
    new_right = decay_rate * right_stats + (1.0 - decay_rate) * right_gram[None]
    return (new_left, new_right, update)


def solution(mesh):
    placed = (
        P("dp", None, "tensor"),
        P("dp", None),
        P("dp", None, "tensor", None),
        P("dp", None, "tensor", None),
        P("dp", None, "tensor", None),
        P("dp", None, None, None),
        P(),
        P(),
    )
    return jax.shard_map(
        body,
        mesh=mesh,
        in_specs=placed,
        out_specs=(
            P("dp", None, "tensor", None),
            P("dp", None, "tensor", None),
            P(("tensor", "dp"), None, None),
        ),
        check_vma=False,
    )
```

```python
import functools

import jax
import jax.numpy as jnp
from jax import lax
from jax.experimental import pallas as pl
from jax.experimental.pallas import tpu as pltpu
from jax.sharding import PartitionSpec as P

decay_rate = 0.99
epsilon = 1e-06

NY, NZ = 4, 8
NX = 4
N_DP = NY * NZ
N_T = NX * 2
BL = 1024
ROWS = 128
NRB, NCB = 4, 10
NB = NRB * NCB
TOK = 128
CW = BL // N_DP
GROWS = NCB * CW
GX = GROWS // NX
SPAN = 3
TA = 80
TAH = 48
TB = TOK - TA
TBH = 32
HALF = N_DP // 2

MESH = pl.DeviceIdType.MESH


def remote(src, dst, send_sem, recv_sem, device):
    return pltpu.make_async_remote_copy(
        src_ref=src,
        dst_ref=dst,
        send_sem=send_sem,
        recv_sem=recv_sem,
        device_id=device,
        device_id_type=MESH,
    )


def await_bytes(ref, sem):
    pltpu.make_async_copy(ref, ref, sem).wait()


def kernel(
    x_hbm,
    g_hbm,
    lr_hbm,
    rr_hbm,
    listed,
    counts,
    nl_out,
    nr_out,
    up_out,
    xall,
    gin,
    gsend,
    gt,
    acc,
    tiles,
    sbuf,
    bt,
    lhs,
    rr,
    pre,
    norms,
    pbuf,
    rv,
    slot_of,
    load_sem,
    greet_sem,
    sent,
    az_sem,
    ay_sem,
    ay2_sem,
    by_sem,
    bz_sem,
    gs_sem,
    gr_sem,
    gx_sem,
    gc_sem,
    ss_sem,
    sr_sem,
    bx_sem,
    bc_sem,
    nsend_sem,
    nr_sem,
    ps_sem,
    pr_sem,
):
    g = lax.axis_index("dp")
    t = lax.axis_index("tensor")
    y, z = g // NZ, g % NZ
    x, core = t // 2, t % 2
    yp, ym = (y + 1) % NY, (y + NY - 1) % NY
    zp, zm = (z + 1) % NZ, (z + NZ - 1) % NZ
    xp, xm = (x + 1) % NX, (x + NX - 1) % NX
    dev_yp, dev_ym = (yp * NZ + z, t), (ym * NZ + z, t)
    dev_zp, dev_zm = (y * NZ + zp, t), (y * NZ + zm, t)
    dev_xp, dev_xm = (g, xp * 2 + core), (g, xm * 2 + core)
    dev_c = (g, x * 2 + 1 - core)
    lane_t = pl.multiple_of(t * ROWS, ROWS)
    both_ways = (True, False)

    barrier = pltpu.get_barrier_semaphore()
    z_line = [(y * NZ + (z + k) % NZ, t) for k in range(1, NZ)]
    y_line = [((y + k) % NY * NZ + z, t) for k in range(1, NY)]
    near = z_line + y_line + [dev_xp, dev_xm, dev_c]
    for device in near:
        pl.semaphore_signal(barrier, inc=1, device_id=device, device_id_type=MESH)

    j0 = (5 * x) // 2
    load_g = pltpu.make_async_copy(
        g_hbm.at[:, pl.ds(pl.multiple_of(j0 * BL, BL), SPAN * BL)], gin, load_sem.at[1]
    )
    load_g.start()
    own_x = pltpu.make_async_copy(x_hbm, xall.at[y, z], load_sem.at[0])
    own_x.start()
    later = [
        pltpu.make_async_copy(lr_hbm, lhs.at[:, pl.ds(ROWS, ROWS)], load_sem.at[2]),
        pltpu.make_async_copy(rr_hbm, rr, load_sem.at[3]),
    ]
    load_g.wait()
    sends_g = core == y // 2

    @pl.when(sends_g)
    def _():
        for j in range(SPAN):
            block = gin[:, j * BL : (j + 1) * BL].T
            gsend[:, j * CW : (j + 1) * CW, :] = block.reshape(N_DP, CW, TOK)

    own_x.wait()
    pl.semaphore_wait(barrier, len(near))

    z_off = (0, NZ - 1, 1, NZ - 2, 2, NZ - 3, 3, 4)

    def az(k, right):
        zs = (z + NZ - k) % NZ if right else (z + k) % NZ
        if k < 3:
            rows = pl.ds(0, TA)
        else:
            rows = pl.ds(0, TAH) if right else pl.ds(TAH, TA - TAH)
        ref = xall.at[y, zs, rows]
        n = k * 2 + (0 if right else 1)
        return remote(ref, ref, sent.at[n], az_sem.at[n], dev_zp if right else dev_zm)

    def ay(p, right):
        ref = xall.at[y, (z + z_off[p]) % NZ, pl.ds(0, TA)]
        n = p * 2 + (0 if right else 1)
        return remote(ref, ref, sent.at[8 + n], ay_sem.at[n], dev_yp if right else dev_ym)

    def ay2(p):
        right = p % 2 == 0
        ref = xall.at[ym if right else yp, (z + z_off[p]) % NZ, pl.ds(0, TA)]
        return remote(ref, ref, sent.at[24 + p], ay2_sem.at[p], dev_yp if right else dev_ym)

    def by(k, right):
        if k == 0:
            ys, rows = y, pl.ds(TA, TB)
        elif right:
            ys, rows = ym, pl.ds(TA, TBH)
        else:
            ys, rows = yp, pl.ds(TA + TBH, TB - TBH)
        ref = xall.at[ys, z, rows]
        n = k * 2 + (0 if right else 1)
        return remote(ref, ref, sent.at[32 + n], by_sem.at[n], dev_yp if right else dev_ym)

    def bz(q, k, right):
        ys = (y, ym, yp, (y + 2) % NY)[q]
        zs = (z + NZ - k) % NZ if right else (z + k) % NZ
        if k < 3:
            rows = pl.ds(TA, TB)
        else:
            rows = pl.ds(TA, TBH) if right else pl.ds(TA + TBH, TB - TBH)
        ref = xall.at[ys, zs, rows]
        n = q * 8 + k * 2 + (0 if right else 1)
        return remote(ref, ref, sent.at[36 + n], bz_sem.at[n], dev_zp if right else dev_zm)

    def az_step(k):
        for right in both_ways:
            az(k - 1, right).wait_recv()
            az(k, right).start()
            p = 2 * k - 1 if right else 2 * k
            for way in both_ways:
                ay(p, way).start()

    def bz_step(q, k):
        for right in both_ways:
            if k:
                bz(q, k - 1, right).wait_recv()
            bz(q, k, right).start()

    def ay2_step(p):
        ay(p, p % 2 == 0).wait_recv()
        ay2(p).start()

    for right in both_ways:
        az(0, right).start()
    for right in both_ways:
        by(0, right).start()

    for device in y_line:
        pl.semaphore_signal(greet_sem, inc=1, device_id=device, device_id_type=MESH)

    offset = pl.multiple_of(((5 * x) % 2) * 16, 16)
    gx_rows = pl.ds(pl.multiple_of(x * GX, 16), GX)
    own_lanes = pl.ds(pl.multiple_of(g * TOK, TOK), TOK)

    def send_g(to):
        remote(
            gsend.at[to, pl.ds(offset, GX)], gt.at[gx_rows, own_lanes], gs_sem, gr_sem, (to, t)
        ).start()

    @pl.when(sends_g)
    def _():
        pltpu.make_async_copy(
            gsend.at[g, pl.ds(offset, GX)], gt.at[gx_rows, own_lanes], gr_sem
        ).start()
        for k in range(1, NZ):
            send_g(y * NZ + (z + k) % NZ)

    for right in both_ways:
        ay(0, right).start()
    pl.semaphore_wait(greet_sem, len(y_line))

    def send_g_row(k):
        @pl.when(sends_g)
        def _():
            for n in range(NZ):
                send_g((y + k) % NY * NZ + (z + n) % NZ)

    half_lanes = pl.ds(pl.multiple_of(core * HALF * TOK, HALF * TOK), HALF * TOK)
    other_lanes = pl.ds(pl.multiple_of((1 - core) * HALF * TOK, HALF * TOK), HALF * TOK)

    quarter = HALF * TOK // 2

    def gxc(k, right):
        xs = x if k < 2 else (xm if right else xp)
        first = right if k != 1 else not right
        rows = pl.ds(pl.multiple_of(xs * GX, 16), GX)
        start = core * HALF * TOK + (0 if first else quarter)
        ref = gt.at[rows, pl.ds(pl.multiple_of(start, quarter), quarter)]
        n = k * 2 + (0 if right else 1)
        return remote(ref, ref, sent.at[68 + n], gx_sem.at[n], dev_xp if right else dev_xm)

    def gcc(step):
        rows = pl.ds(pl.multiple_of((x + NX - step) % NX * GX, 16), GX)
        ref = gt.at[rows, half_lanes]
        return remote(ref, ref, sent.at[74 + step], gc_sem.at[step], dev_c)

    def step_by():
        for right in both_ways:
            by(0, right).wait_recv()
        for right in both_ways:
            by(1, right).start()

    def step_by1():
        for right in both_ways:
            by(1, right).wait_recv()

    def step_G0():
        await_bytes(gt.at[gx_rows, half_lanes], gr_sem)
        for k in range(2):
            for right in both_ways:
                gxc(k, right).start()
        gcc(0).start()

    def step_G1():
        for right in both_ways:
            gxc(0, right).wait_recv()
            gxc(2, right).start()
        for right in both_ways:
            gxc(1, right).wait_recv()
            gcc(1 if right else 3).start()

    def step_G2():
        for right in both_ways:
            gxc(2, right).wait_recv()
        gcc(2).start()

    def step_ay7():
        for right in both_ways:
            az(3, right).wait_recv()
        for right in both_ways:
            ay(7, right).start()

    def step_L():
        for copy in later:
            copy.start()

    az_step(1)
    send_g_row(1)
    step_by()
    send_g_row(2)
    az_step(2)
    send_g_row(3)
    bz_step(0, 0)
    ay2_step(0)
    bz_step(1, 0)
    bz_step(2, 0)
    az_step(3)
    step_L()
    ay2_step(1)
    ay2_step(2)
    bz_step(0, 1)
    step_by1()
    bz_step(3, 0)
    step_G0()
    bz_step(1, 1)
    bz_step(2, 1)
    step_ay7()
    ay2_step(3)
    ay2_step(4)
    bz_step(0, 2)
    bz_step(3, 1)
    ay2_step(5)
    ay2_step(6)
    bz_step(1, 2)
    bz_step(2, 2)
    step_G1()
    bz_step(0, 3)
    bz_step(3, 2)
    ay2_step(7)
    bz_step(1, 3)
    bz_step(2, 3)
    bz_step(3, 3)
    step_G2()

    def add_tokens(ys):
        lanes = pl.ds(pl.multiple_of(ys * NZ * TOK, NZ * TOK), NZ * TOK)
        part = xall[ys].reshape(NZ * TOK, NRB * ROWS)
        return jnp.dot(gt[:, lanes], part, preferred_element_type=jnp.float32)

    for step in (0, 1, 3, 2):
        gcc(step).wait_recv()
    for right in both_ways:
        bz(0, 3, right).wait_recv()
    acc[...] = add_tokens(y)
    for p in range(NZ):
        ay(p, p % 2 == 1).wait_recv()
    for q in (1, 2):
        for right in both_ways:
            bz(q, 3, right).wait_recv()
    acc[...] += add_tokens(ym)
    acc[...] += add_tokens(yp)
    for p in range(NZ):
        ay2(p).wait_recv()
    for right in both_ways:
        bz(3, 3, right).wait_recv()
    acc[...] += add_tokens((y + 2) % NY)
    for i in range(NRB):
        for j in range(NCB):
            tiles[i * NCB + j] = acc[
                j * CW : (j + 1) * CW, i * ROWS : (i + 1) * ROWS
            ].astype(jnp.bfloat16)
    tiles[NB] = jnp.zeros((CW, ROWS), jnp.bfloat16)

    bt_rows = pl.ds(pl.multiple_of(g * CW, CW), CW)
    bt_lanes = pl.ds(lane_t, ROWS)
    def listed_block(to, s):
        block = jnp.clip(listed[to * 2 + s], 0, NB - 1)
        return jnp.where(s < counts[to], block, NB)

    def send_blocks(s):
        def send_block(d, carry):
            to = (g + d) % N_DP
            sbuf[s, to] = tiles[listed_block(to, s)]
            remote(
                sbuf.at[s, to], bt.at[s, bt_rows, bt_lanes], ss_sem.at[s], sr_sem.at[s], (to, t)
            ).start()
            return carry

        sbuf[s, g] = tiles[listed_block(g, s)]
        pltpu.make_async_copy(sbuf.at[s, g], bt.at[s, bt_rows, bt_lanes], sr_sem.at[s]).start()
        lax.fori_loop(1, N_DP, send_block, 0)

    def lanes_of(xs, cs):
        return pl.ds(pl.multiple_of((xs * 2 + cs) * ROWS, ROWS), ROWS)

    def bxc(s, k, right):
        xs = x if k < 2 else (xm if right else xp)
        first = right if k != 1 else not right
        rows = pl.ds(0 if first else BL // 2, BL // 2)
        ref = bt.at[s, rows, lanes_of(xs, core)]
        n = s * 6 + k * 2 + (0 if right else 1)
        return remote(ref, ref, sent.at[78 + n], bx_sem.at[n], dev_xp if right else dev_xm)

    def bcc(s, step):
        ref = bt.at[s, :, lanes_of((x + NX - step) % NX, core)]
        n = s * 4 + step
        return remote(ref, ref, sent.at[90 + n], bc_sem.at[n], dev_c)

    def gather_start(s):
        await_bytes(bt.at[s, :, bt_lanes], sr_sem.at[s])
        for k in range(2):
            for right in both_ways:
                bxc(s, k, right).start()
        bcc(s, 0).start()
        own = bt[s, :, bt_lanes].astype(jnp.float32)
        norms[s, t, 0:8] = jnp.sum((own * own).reshape(-1, 8, ROWS), axis=0)

    def gather_middle(s):
        for right in both_ways:
            bxc(s, 0, right).wait_recv()
            bxc(s, 2, right).start()
        for right in both_ways:
            bxc(s, 1, right).wait_recv()
            bcc(s, 1 if right else 3).start()

    def gather_end(s):
        for right in both_ways:
            bxc(s, 2, right).wait_recv()
        bcc(s, 2).start()
        for step in (0, 1, 3, 2):
            bcc(s, step).wait_recv()

    def norm_copy(s, d):
        ref = norms.at[s, t]
        return remote(ref, ref, nsend_sem.at[s], nr_sem.at[s, d], (g, (t + d) % N_T))

    def precondition(s):
        lhs[s, 0:ROWS] = bt[s, pl.ds(lane_t, ROWS), :]
        both = lax.dot_general(
            lhs[s], bt[s], (((1,), (1,)), ((), ())), preferred_element_type=jnp.float32
        )
        nr_out[s] = both[0:ROWS]
        applied = both[ROWS:].astype(jnp.bfloat16)
        precond = jnp.dot(applied, rr[s], preferred_element_type=jnp.float32)
        pre[s] = precond
        squares = precond * precond
        folded = jnp.sum(squares.reshape(-1, 8, BL), axis=0)
        total = folded[:, 0:ROWS]
        for m in range(1, BL // ROWS):
            total = total + folded[:, m * ROWS : (m + 1) * ROWS]
        norms[s, t, 8:16] = total
        for d in range(1, N_T):
            norm_copy(s, d).start()

    def send_rows(s):
        for d in range(1, N_T):
            norm_copy(s, d).wait_recv()
        sums = jnp.sum(norms[s], axis=0)
        grad_sq = jnp.sum(sums[0:8], keepdims=True)
        prec_sq = jnp.sum(sums[8:16], keepdims=True)
        scale = jnp.sqrt(grad_sq) * lax.rsqrt(prec_sq + epsilon)
        grafted = pre[s] * scale
        pbuf[s] = grafted.reshape(ROWS, 8, ROWS).reshape(N_DP, 32, ROWS).astype(jnp.bfloat16)
        pltpu.make_async_copy(pbuf.at[s, g], rv.at[s, g], pr_sem.at[s]).start()

        def send_back(d, carry):
            to = (g + d) % N_DP
            remote(pbuf.at[s, to], rv.at[s, g], ps_sem.at[s], pr_sem.at[s], (to, t)).start()
            return carry

        lax.fori_loop(1, N_DP, send_back, 0)

    def left(s):
        own = bt[s, :, bt_lanes]
        nl_out[s] = lax.dot_general(
            own, bt[s], (((0,), (0,)), ((), ())), preferred_element_type=jnp.float32
        )

    send_blocks(0)
    gather_start(0)
    send_blocks(1)
    gather_middle(0)
    gather_start(1)
    for copy in later:
        copy.wait()
    gather_end(0)
    precondition(0)
    gather_middle(1)
    left(0)
    send_rows(0)
    gather_end(1)
    precondition(1)
    left(1)
    send_rows(1)

    for k in range(4):
        for right in both_ways:
            az(k, right).wait_send()
            for q in range(NY):
                bz(q, k, right).wait_send()
    for p in range(NZ):
        for right in both_ways:
            ay(p, right).wait_send()
        ay2(p).wait_send()
    for right in both_ways:
        for k in range(2):
            by(k, right).wait_send()
        for k in range(3):
            gxc(k, right).wait_send()
    for step in range(4):
        gcc(step).wait_send()

    @pl.when(sends_g)
    def _():
        await_bytes(gsend.at[pl.ds(0, N_DP - 1), pl.ds(0, GX)], gs_sem)

    for s in range(2):
        await_bytes(sbuf.at[s, pl.ds(0, N_DP - 1)], ss_sem.at[s])
        for k in range(3):
            for right in both_ways:
                bxc(s, k, right).wait_send()
        for step in range(4):
            bcc(s, step).wait_send()
        await_bytes(norms.at[s, pl.ds(0, N_T - 1)], nsend_sem.at[s])
        await_bytes(pbuf.at[s, pl.ds(0, N_DP - 1)], ps_sem.at[s])

    lane = lax.broadcasted_iota(jnp.int32, (8, ROWS), 1)
    slots = jnp.zeros((8, ROWS), jnp.int32)
    for slot in range(2 * N_DP):
        slots = jnp.where(lane == listed_block(slot // 2, slot % 2), slot, slots)
    for b in range(NB):
        slot_of[b] = jnp.max(jnp.where(lane == b, slots, 0))

    for s in range(2):
        await_bytes(rv.at[s], pr_sem.at[s])

    def place(b, carry):
        slot = slot_of[b]
        rows = rv[slot % 2, slot // 2]
        for k in range(4):
            up_out[k, b] = rows[k * 8 : (k + 1) * 8]
        return carry

    lax.fori_loop(0, NB, place, 0)

def body(
    layer_inputs,
    output_grads,
    left_stats,
    right_stats,
    left_roots,
    right_roots,
    owner_blocks,
    block_counts,
):
    f32, bf16 = jnp.float32, jnp.bfloat16
    dma = pltpu.SemaphoreType.DMA
    hbm = pl.BlockSpec(memory_space=pltpu.HBM)
    vmem = pl.BlockSpec(memory_space=pltpu.VMEM)
    smem = pl.BlockSpec(memory_space=pltpu.SMEM)
    left_gram, right_gram, update = pl.pallas_call(
        kernel,
        out_shape=(
            jax.ShapeDtypeStruct((2, ROWS, BL), f32),
            jax.ShapeDtypeStruct((2, ROWS, BL), f32),
            jax.ShapeDtypeStruct((4, NB, 8, ROWS), bf16),
        ),
        in_specs=[hbm] * 4 + [smem] * 2,
        out_specs=(vmem, vmem, vmem),
        scratch_shapes=[
            pltpu.VMEM((NY, NZ, TOK, NRB * ROWS), bf16),
            pltpu.VMEM((TOK, SPAN * BL), bf16),
            pltpu.VMEM((N_DP, SPAN * CW, TOK), bf16),
            pltpu.VMEM((GROWS, N_DP * TOK), bf16),
            pltpu.VMEM((GROWS, NRB * ROWS), f32),
            pltpu.VMEM((NB + 1, CW, ROWS), bf16),
            pltpu.VMEM((2, N_DP, CW, ROWS), bf16),
            pltpu.VMEM((2, BL, BL), bf16),
            pltpu.VMEM((2, 2 * ROWS, BL), bf16),
            pltpu.VMEM((2, BL, BL), bf16),
            pltpu.VMEM((2, ROWS, BL), f32),
            pltpu.VMEM((2, N_T, 16, ROWS), f32),
            pltpu.VMEM((2, N_DP, 32, ROWS), bf16),
            pltpu.VMEM((2, N_DP, 32, ROWS), bf16),
            pltpu.SMEM((NB,), jnp.int32),
            dma((4,)),
            pltpu.SemaphoreType.REGULAR,
            dma((98,)),
            dma((8,)),
            dma((16,)),
            dma((8,)),
            dma((4,)),
            dma((32,)),
            dma,
            dma,
            dma((6,)),
            dma((4,)),
            dma((2,)),
            dma((2,)),
            dma((12,)),
            dma((8,)),
            dma((2,)),
            dma((2, N_T)),
            dma((2,)),
            dma((2,)),
        ],
        compiler_params=pltpu.CompilerParams(
            collective_id=0, has_side_effects=True, vmem_limit_bytes=48 * 1024 * 1024
        ),
        cost_estimate=pl.CostEstimate(
            flops=4_000_000_000, bytes_accessed=16_000_000, transcendentals=0
        ),
    )(
        layer_inputs.reshape(TOK, NRB * ROWS),
        output_grads,
        left_roots[0],
        right_roots[0],
        owner_blocks.reshape(-1),
        block_counts,
    )
    update = update.reshape(4, NRB, NCB * BL)
    new_left = decay_rate * left_stats + (1.0 - decay_rate) * left_gram[None]
    new_right = decay_rate * right_stats + (1.0 - decay_rate) * right_gram[None]
    return (new_left, new_right, update)


def solution(mesh):
    placed = (
        P("dp", None, "tensor"),
        P("dp", None),
        P("dp", None, "tensor", None),
        P("dp", None, "tensor", None),
        P("dp", None, "tensor", None),
        P("dp", None, None, None),
        P(),
        P(),
    )
    return jax.shard_map(
        body,
        mesh=mesh,
        in_specs=placed,
        out_specs=(
            P("dp", None, "tensor", None),
            P("dp", None, "tensor", None),
            P(("tensor", "dp"), None, None),
        ),
        check_vma=False,
    )
```

```python
import functools

import jax
import jax.numpy as jnp
from jax import lax
from jax.experimental import pallas as pl
from jax.experimental.pallas import tpu as pltpu
from jax.sharding import PartitionSpec as P

decay_rate = 0.99
epsilon = 1e-06

NY, NZ = 4, 8
NX = 4
N_DP = NY * NZ
N_T = NX * 2
BL = 1024
ROWS = 128
NRB, NCB = 4, 10
NB = NRB * NCB
TOK = 128
CW = BL // N_DP
GROWS = NCB * CW
GX = GROWS // NX
SPAN = 3
TA = 80
TAH = 48
TB = TOK - TA
TBH = 32
HALF = N_DP // 2

MESH = pl.DeviceIdType.MESH


def remote(src, dst, send_sem, recv_sem, device):
    return pltpu.make_async_remote_copy(
        src_ref=src,
        dst_ref=dst,
        send_sem=send_sem,
        recv_sem=recv_sem,
        device_id=device,
        device_id_type=MESH,
    )


def await_bytes(ref, sem):
    pltpu.make_async_copy(ref, ref, sem).wait()


def kernel(
    x_hbm,
    g_hbm,
    lr_hbm,
    rr_hbm,
    listed,
    nl_out,
    nr_out,
    up_out,
    xall,
    gin,
    gsend,
    gt,
    acc,
    tiles,
    sbuf,
    bt,
    lhs,
    rr,
    pre,
    norms,
    pbuf,
    rv,
    slot_of,
    load_sem,
    greet_sem,
    sent,
    az_sem,
    ay_sem,
    ay2_sem,
    by_sem,
    bz_sem,
    gs_sem,
    gr_sem,
    gx_sem,
    gc_sem,
    ss_sem,
    sr_sem,
    bx_sem,
    bc_sem,
    nsend_sem,
    nr_sem,
    ps_sem,
    pr_sem,
):
    g = lax.axis_index("dp")
    t = lax.axis_index("tensor")
    y, z = g // NZ, g % NZ
    x, core = t // 2, t % 2
    yp, ym = (y + 1) % NY, (y + NY - 1) % NY
    zp, zm = (z + 1) % NZ, (z + NZ - 1) % NZ
    xp, xm = (x + 1) % NX, (x + NX - 1) % NX
    dev_yp, dev_ym = (yp * NZ + z, t), (ym * NZ + z, t)
    dev_zp, dev_zm = (y * NZ + zp, t), (y * NZ + zm, t)
    dev_xp, dev_xm = (g, xp * 2 + core), (g, xm * 2 + core)
    dev_c = (g, x * 2 + 1 - core)
    lane_t = pl.multiple_of(t * ROWS, ROWS)
    both_ways = (True, False)

    barrier = pltpu.get_barrier_semaphore()
    z_line = [(y * NZ + (z + k) % NZ, t) for k in range(1, NZ)]
    y_line = [((y + k) % NY * NZ + z, t) for k in range(1, NY)]
    near = z_line + y_line + [dev_xp, dev_xm, dev_c]
    for device in near:
        pl.semaphore_signal(barrier, inc=1, device_id=device, device_id_type=MESH)

    j0 = (5 * x) // 2
    load_g = pltpu.make_async_copy(
        g_hbm.at[:, pl.ds(pl.multiple_of(j0 * BL, BL), SPAN * BL)], gin, load_sem.at[1]
    )
    load_g.start()
    own_x = pltpu.make_async_copy(x_hbm, xall.at[y, z], load_sem.at[0])
    own_x.start()
    later = [
        pltpu.make_async_copy(lr_hbm, lhs.at[:, pl.ds(ROWS, ROWS)], load_sem.at[2]),
        pltpu.make_async_copy(rr_hbm, rr, load_sem.at[3]),
    ]
    load_g.wait()
    sends_g = core == y // 2

    @pl.when(sends_g)
    def _():
        for j in range(SPAN):
            block = gin[:, j * BL : (j + 1) * BL].T
            gsend[:, j * CW : (j + 1) * CW, :] = block.reshape(N_DP, CW, TOK)

    own_x.wait()
    pl.semaphore_wait(barrier, len(near))

    z_off = (0, NZ - 1, 1, NZ - 2, 2, NZ - 3, 3, 4)

    def az(k, right):
        zs = (z + NZ - k) % NZ if right else (z + k) % NZ
        if k < 3:
            rows = pl.ds(0, TA)
        else:
            rows = pl.ds(0, TAH) if right else pl.ds(TAH, TA - TAH)
        ref = xall.at[y, zs, rows]
        n = k * 2 + (0 if right else 1)
        return remote(ref, ref, sent.at[n], az_sem.at[n], dev_zp if right else dev_zm)

    def ay(p, right):
        ref = xall.at[y, (z + z_off[p]) % NZ, pl.ds(0, TA)]
        n = p * 2 + (0 if right else 1)
        return remote(ref, ref, sent.at[8 + n], ay_sem.at[n], dev_yp if right else dev_ym)

    def ay2(p):
        right = p % 2 == 0
        ref = xall.at[ym if right else yp, (z + z_off[p]) % NZ, pl.ds(0, TA)]
        return remote(ref, ref, sent.at[24 + p], ay2_sem.at[p], dev_yp if right else dev_ym)

    def by(k, right):
        if k == 0:
            ys, rows = y, pl.ds(TA, TB)
        elif right:
            ys, rows = ym, pl.ds(TA, TBH)
        else:
            ys, rows = yp, pl.ds(TA + TBH, TB - TBH)
        ref = xall.at[ys, z, rows]
        n = k * 2 + (0 if right else 1)
        return remote(ref, ref, sent.at[32 + n], by_sem.at[n], dev_yp if right else dev_ym)

    def bz(q, k, right):
        ys = (y, ym, yp, (y + 2) % NY)[q]
        zs = (z + NZ - k) % NZ if right else (z + k) % NZ
        if k < 3:
            rows = pl.ds(TA, TB)
        else:
            rows = pl.ds(TA, TBH) if right else pl.ds(TA + TBH, TB - TBH)
        ref = xall.at[ys, zs, rows]
        n = q * 8 + k * 2 + (0 if right else 1)
        return remote(ref, ref, sent.at[36 + n], bz_sem.at[n], dev_zp if right else dev_zm)

    def az_step(k):
        for right in both_ways:
            az(k - 1, right).wait_recv()
            az(k, right).start()
            p = 2 * k - 1 if right else 2 * k
            for way in both_ways:
                ay(p, way).start()

    def bz_step(q, k):
        for right in both_ways:
            if k:
                bz(q, k - 1, right).wait_recv()
            bz(q, k, right).start()

    def ay2_step(p):
        ay(p, p % 2 == 0).wait_recv()
        ay2(p).start()

    for right in both_ways:
        az(0, right).start()
    for right in both_ways:
        by(0, right).start()

    for device in y_line:
        pl.semaphore_signal(greet_sem, inc=1, device_id=device, device_id_type=MESH)

    offset = pl.multiple_of(((5 * x) % 2) * 16, 16)
    gx_rows = pl.ds(pl.multiple_of(x * GX, 16), GX)
    own_lanes = pl.ds(pl.multiple_of(g * TOK, TOK), TOK)

    def send_g(to):
        remote(
            gsend.at[to, pl.ds(offset, GX)], gt.at[gx_rows, own_lanes], gs_sem, gr_sem, (to, t)
        ).start()

    @pl.when(sends_g)
    def _():
        pltpu.make_async_copy(
            gsend.at[g, pl.ds(offset, GX)], gt.at[gx_rows, own_lanes], gr_sem
        ).start()
        for k in range(1, NZ):
            send_g(y * NZ + (z + k) % NZ)

    for right in both_ways:
        ay(0, right).start()
    pl.semaphore_wait(greet_sem, len(y_line))

    def send_g_row(k):
        @pl.when(sends_g)
        def _():
            for n in range(NZ):
                send_g((y + k) % NY * NZ + (z + n) % NZ)

    half_lanes = pl.ds(pl.multiple_of(core * HALF * TOK, HALF * TOK), HALF * TOK)
    other_lanes = pl.ds(pl.multiple_of((1 - core) * HALF * TOK, HALF * TOK), HALF * TOK)

    quarter = HALF * TOK // 2

    def gxc(k, right):
        xs = x if k < 2 else (xm if right else xp)
        first = right if k != 1 else not right
        rows = pl.ds(pl.multiple_of(xs * GX, 16), GX)
        start = core * HALF * TOK + (0 if first else quarter)
        ref = gt.at[rows, pl.ds(pl.multiple_of(start, quarter), quarter)]
        n = k * 2 + (0 if right else 1)
        return remote(ref, ref, sent.at[68 + n], gx_sem.at[n], dev_xp if right else dev_xm)

    def gcc(step):
        rows = pl.ds(pl.multiple_of((x + NX - step) % NX * GX, 16), GX)
        ref = gt.at[rows, half_lanes]
        return remote(ref, ref, sent.at[74 + step], gc_sem.at[step], dev_c)

    def step_by():
        for right in both_ways:
            by(0, right).wait_recv()
        for right in both_ways:
            by(1, right).start()

    def step_by1():
        for right in both_ways:
            by(1, right).wait_recv()

    def step_G0():
        await_bytes(gt.at[gx_rows, half_lanes], gr_sem)
        for k in range(2):
            for right in both_ways:
                gxc(k, right).start()
        gcc(0).start()

    def step_G1():
        for right in both_ways:
            gxc(0, right).wait_recv()
            gxc(2, right).start()
        for right in both_ways:
            gxc(1, right).wait_recv()
            gcc(1 if right else 3).start()

    def step_G2():
        for right in both_ways:
            gxc(2, right).wait_recv()
        gcc(2).start()

    def step_ay7():
        for right in both_ways:
            az(3, right).wait_recv()
        for right in both_ways:
            ay(7, right).start()

    def step_L():
        for copy in later:
            copy.start()

    az_step(1)
    send_g_row(1)
    step_by()
    send_g_row(2)
    az_step(2)
    send_g_row(3)
    bz_step(0, 0)
    ay2_step(0)
    bz_step(1, 0)
    bz_step(2, 0)
    az_step(3)
    step_L()
    ay2_step(1)
    ay2_step(2)
    bz_step(0, 1)
    step_by1()
    bz_step(3, 0)
    step_G0()
    bz_step(1, 1)
    bz_step(2, 1)
    step_ay7()
    ay2_step(3)
    ay2_step(4)
    bz_step(0, 2)
    bz_step(3, 1)
    ay2_step(5)
    ay2_step(6)
    bz_step(1, 2)
    bz_step(2, 2)
    step_G1()
    bz_step(0, 3)
    bz_step(3, 2)
    ay2_step(7)
    bz_step(1, 3)
    bz_step(2, 3)
    bz_step(3, 3)
    step_G2()

    def add_tokens(ys):
        lanes = pl.ds(pl.multiple_of(ys * NZ * TOK, NZ * TOK), NZ * TOK)
        part = xall[ys].reshape(NZ * TOK, NRB * ROWS)
        return jnp.dot(gt[:, lanes], part, preferred_element_type=jnp.float32)

    for step in (0, 1, 3, 2):
        gcc(step).wait_recv()
    for right in both_ways:
        bz(0, 3, right).wait_recv()
    acc[...] = add_tokens(y)
    for p in range(NZ):
        ay(p, p % 2 == 1).wait_recv()
    for q in (1, 2):
        for right in both_ways:
            bz(q, 3, right).wait_recv()
    acc[...] += add_tokens(ym)
    acc[...] += add_tokens(yp)
    for p in range(NZ):
        ay2(p).wait_recv()
    for right in both_ways:
        bz(3, 3, right).wait_recv()
    acc[...] += add_tokens((y + 2) % NY)
    for i in range(NRB):
        for j in range(NCB):
            tiles[i * NCB + j] = acc[
                j * CW : (j + 1) * CW, i * ROWS : (i + 1) * ROWS
            ].astype(jnp.bfloat16)
    tiles[NB] = jnp.zeros((CW, ROWS), jnp.bfloat16)

    bt_rows = pl.ds(pl.multiple_of(g * CW, CW), CW)
    bt_lanes = pl.ds(lane_t, ROWS)
    def listed_block(to, s):
        return listed[s, to]

    def send_blocks(s):
        def send_block(d):
            to = (g + d) % N_DP
            sbuf[s, to] = tiles[listed_block(to, s)]
            remote(
                sbuf.at[s, to], bt.at[s, bt_rows, bt_lanes], ss_sem.at[s], sr_sem.at[s], (to, t)
            ).start()

        sbuf[s, g] = tiles[listed_block(g, s)]
        pltpu.make_async_copy(sbuf.at[s, g], bt.at[s, bt_rows, bt_lanes], sr_sem.at[s]).start()
        for d in range(1, N_DP):
            send_block(d)

    def lanes_of(xs, cs):
        return pl.ds(pl.multiple_of((xs * 2 + cs) * ROWS, ROWS), ROWS)

    def bxc(s, k, right):
        xs = x if k < 2 else (xm if right else xp)
        first = right if k != 1 else not right
        rows = pl.ds(0 if first else BL // 2, BL // 2)
        ref = bt.at[s, rows, lanes_of(xs, core)]
        n = s * 6 + k * 2 + (0 if right else 1)
        return remote(ref, ref, sent.at[78 + n], bx_sem.at[n], dev_xp if right else dev_xm)

    def bcc(s, step):
        ref = bt.at[s, :, lanes_of((x + NX - step) % NX, core)]
        n = s * 4 + step
        return remote(ref, ref, sent.at[90 + n], bc_sem.at[n], dev_c)

    def gather_start(s):
        await_bytes(bt.at[s, :, bt_lanes], sr_sem.at[s])
        for k in range(2):
            for right in both_ways:
                bxc(s, k, right).start()
        bcc(s, 0).start()
        own = bt[s, :, bt_lanes].astype(jnp.float32)
        norms[s, t, 0:8] = jnp.sum((own * own).reshape(-1, 8, ROWS), axis=0)

    def gather_middle(s):
        for right in both_ways:
            bxc(s, 0, right).wait_recv()
            bxc(s, 2, right).start()
        for right in both_ways:
            bxc(s, 1, right).wait_recv()
            bcc(s, 1 if right else 3).start()

    def gather_end(s):
        for right in both_ways:
            bxc(s, 2, right).wait_recv()
        bcc(s, 2).start()
        for step in (0, 1, 3, 2):
            bcc(s, step).wait_recv()

    def norm_copy(s, d):
        ref = norms.at[s, t]
        return remote(ref, ref, nsend_sem.at[s], nr_sem.at[s, d], (g, (t + d) % N_T))

    def precondition(s):
        lhs[s, 0:ROWS] = bt[s, pl.ds(lane_t, ROWS), :]
        both = lax.dot_general(
            lhs[s], bt[s], (((1,), (1,)), ((), ())), preferred_element_type=jnp.float32
        )
        nr_out[s] = both[0:ROWS]
        applied = both[ROWS:].astype(jnp.bfloat16)
        precond = jnp.dot(applied, rr[s], preferred_element_type=jnp.float32)
        pre[s] = precond
        squares = precond * precond
        folded = jnp.sum(squares.reshape(-1, 8, BL), axis=0)
        total = folded[:, 0:ROWS]
        for m in range(1, BL // ROWS):
            total = total + folded[:, m * ROWS : (m + 1) * ROWS]
        norms[s, t, 8:16] = total
        for d in range(1, N_T):
            norm_copy(s, d).start()

    def send_rows(s):
        for d in range(1, N_T):
            norm_copy(s, d).wait_recv()
        sums = jnp.sum(norms[s], axis=0)
        grad_sq = jnp.sum(sums[0:8], keepdims=True)
        prec_sq = jnp.sum(sums[8:16], keepdims=True)
        scale = jnp.sqrt(grad_sq) * lax.rsqrt(prec_sq + epsilon)
        grafted = pre[s] * scale
        pbuf[s] = grafted.reshape(ROWS, 8, ROWS).reshape(N_DP, 32, ROWS).astype(jnp.bfloat16)
        pltpu.make_async_copy(pbuf.at[s, g], rv.at[s, g], pr_sem.at[s]).start()

        def send_back(d, carry):
            to = (g + d) % N_DP
            remote(pbuf.at[s, to], rv.at[s, g], ps_sem.at[s], pr_sem.at[s], (to, t)).start()
            return carry

        lax.fori_loop(1, N_DP, send_back, 0)

    def left(s):
        own = bt[s, :, bt_lanes]
        nl_out[s] = lax.dot_general(
            own, bt[s], (((0,), (0,)), ((), ())), preferred_element_type=jnp.float32
        )

    send_blocks(0)
    gather_start(0)
    send_blocks(1)
    gather_middle(0)
    gather_start(1)
    for copy in later:
        copy.wait()
    gather_end(0)
    precondition(0)
    gather_middle(1)
    left(0)
    send_rows(0)
    gather_end(1)
    precondition(1)
    left(1)
    send_rows(1)

    for k in range(4):
        for right in both_ways:
            az(k, right).wait_send()
            for q in range(NY):
                bz(q, k, right).wait_send()
    for p in range(NZ):
        for right in both_ways:
            ay(p, right).wait_send()
        ay2(p).wait_send()
    for right in both_ways:
        for k in range(2):
            by(k, right).wait_send()
        for k in range(3):
            gxc(k, right).wait_send()
    for step in range(4):
        gcc(step).wait_send()

    @pl.when(sends_g)
    def _():
        await_bytes(gsend.at[pl.ds(0, N_DP - 1), pl.ds(0, GX)], gs_sem)

    for s in range(2):
        await_bytes(sbuf.at[s, pl.ds(0, N_DP - 1)], ss_sem.at[s])
        for k in range(3):
            for right in both_ways:
                bxc(s, k, right).wait_send()
        for step in range(4):
            bcc(s, step).wait_send()
        await_bytes(norms.at[s, pl.ds(0, N_T - 1)], nsend_sem.at[s])
        await_bytes(pbuf.at[s, pl.ds(0, N_DP - 1)], ps_sem.at[s])

    lane = lax.broadcasted_iota(jnp.int32, (8, ROWS), 1)
    slots = jnp.zeros((8, ROWS), jnp.int32)
    for slot in range(2 * N_DP):
        slots = jnp.where(lane == listed_block(slot % N_DP, slot // N_DP), slot, slots)
    for b in range(NB):
        slot_of[b] = jnp.max(jnp.where(lane == b, slots, 0))

    for s in range(2):
        await_bytes(rv.at[s], pr_sem.at[s])

    for b in range(NB):
        slot = slot_of[b]
        rows = rv[slot // N_DP, slot % N_DP]
        for k in range(4):
            up_out[k, b] = rows[k * 8 : (k + 1) * 8]

def body(
    layer_inputs,
    output_grads,
    left_stats,
    right_stats,
    left_roots,
    right_roots,
    owner_blocks,
    block_counts,
):
    f32, bf16 = jnp.float32, jnp.bfloat16
    live = jnp.arange(2, dtype=jnp.int32)[:, None] < block_counts[None, :]
    listed = jnp.where(live, jnp.clip(owner_blocks.T, 0, NB - 1), NB)
    dma = pltpu.SemaphoreType.DMA
    hbm = pl.BlockSpec(memory_space=pltpu.HBM)
    vmem = pl.BlockSpec(memory_space=pltpu.VMEM)
    smem = pl.BlockSpec(memory_space=pltpu.SMEM)
    left_gram, right_gram, update = pl.pallas_call(
        kernel,
        out_shape=(
            jax.ShapeDtypeStruct((2, ROWS, BL), f32),
            jax.ShapeDtypeStruct((2, ROWS, BL), f32),
            jax.ShapeDtypeStruct((4, NB, 8, ROWS), bf16),
        ),
        in_specs=[hbm] * 4 + [smem],
        out_specs=(vmem, vmem, vmem),
        scratch_shapes=[
            pltpu.VMEM((NY, NZ, TOK, NRB * ROWS), bf16),
            pltpu.VMEM((TOK, SPAN * BL), bf16),
            pltpu.VMEM((N_DP, SPAN * CW, TOK), bf16),
            pltpu.VMEM((GROWS, N_DP * TOK), bf16),
            pltpu.VMEM((GROWS, NRB * ROWS), f32),
            pltpu.VMEM((NB + 1, CW, ROWS), bf16),
            pltpu.VMEM((2, N_DP, CW, ROWS), bf16),
            pltpu.VMEM((2, BL, BL), bf16),
            pltpu.VMEM((2, 2 * ROWS, BL), bf16),
            pltpu.VMEM((2, BL, BL), bf16),
            pltpu.VMEM((2, ROWS, BL), f32),
            pltpu.VMEM((2, N_T, 16, ROWS), f32),
            pltpu.VMEM((2, N_DP, 32, ROWS), bf16),
            pltpu.VMEM((2, N_DP, 32, ROWS), bf16),
            pltpu.SMEM((NB,), jnp.int32),
            dma((4,)),
            pltpu.SemaphoreType.REGULAR,
            dma((98,)),
            dma((8,)),
            dma((16,)),
            dma((8,)),
            dma((4,)),
            dma((32,)),
            dma,
            dma,
            dma((6,)),
            dma((4,)),
            dma((2,)),
            dma((2,)),
            dma((12,)),
            dma((8,)),
            dma((2,)),
            dma((2, N_T)),
            dma((2,)),
            dma((2,)),
        ],
        compiler_params=pltpu.CompilerParams(
            collective_id=0, has_side_effects=True, vmem_limit_bytes=50 * 1024 * 1024
        ),
        cost_estimate=pl.CostEstimate(
            flops=4_000_000_000, bytes_accessed=16_000_000, transcendentals=0
        ),
    )(
        layer_inputs.reshape(TOK, NRB * ROWS),
        output_grads,
        left_roots[0],
        right_roots[0],
        listed,
    )
    update = update.reshape(4, NRB, NCB * BL)
    new_left = decay_rate * left_stats + (1.0 - decay_rate) * left_gram[None]
    new_right = decay_rate * right_stats + (1.0 - decay_rate) * right_gram[None]
    return (new_left, new_right, update)


def solution(mesh):
    placed = (
        P("dp", None, "tensor"),
        P("dp", None),
        P("dp", None, "tensor", None),
        P("dp", None, "tensor", None),
        P("dp", None, "tensor", None),
        P("dp", None, None, None),
        P(),
        P(),
    )
    return jax.shard_map(
        body,
        mesh=mesh,
        in_specs=placed,
        out_specs=(
            P("dp", None, "tensor", None),
            P("dp", None, "tensor", None),
            P(("tensor", "dp"), None, None),
        ),
        check_vma=False,
    )
```

```python
import functools

import jax
import jax.numpy as jnp
from jax import lax
from jax.experimental import pallas as pl
from jax.experimental.pallas import tpu as pltpu
from jax.sharding import PartitionSpec as P

decay_rate = 0.99
epsilon = 1e-06

NY, NZ = 4, 8
NX = 4
N_DP = NY * NZ
N_T = NX * 2
BL = 1024
ROWS = 128
NRB, NCB = 4, 10
NB = NRB * NCB
TOK = 128
CW = BL // N_DP
GROWS = NCB * CW
GX = GROWS // NX
SPAN = 3
TA = 80
TAH = 48
TB = TOK - TA
TBH = 32
HALF = N_DP // 2

MESH = pl.DeviceIdType.MESH


def remote(src, dst, send_sem, recv_sem, device):
    return pltpu.make_async_remote_copy(
        src_ref=src,
        dst_ref=dst,
        send_sem=send_sem,
        recv_sem=recv_sem,
        device_id=device,
        device_id_type=MESH,
    )


def await_bytes(ref, sem):
    pltpu.make_async_copy(ref, ref, sem).wait()


def kernel(
    x_hbm,
    g_hbm,
    lr_hbm,
    rr_hbm,
    listed,
    nl_out,
    nr_out,
    up_out,
    xall,
    gin,
    gsend,
    gt,
    acc,
    tiles,
    sbuf,
    bt,
    lhs,
    rr,
    pre,
    norms,
    pbuf,
    rv,
    slot_of,
    load_sem,
    greet_sem,
    sent,
    az_sem,
    ay_sem,
    ay2_sem,
    by_sem,
    bz_sem,
    gs_sem,
    gr_sem,
    gx_sem,
    gc_sem,
    ss_sem,
    sr_sem,
    bx_sem,
    bc_sem,
    nsend_sem,
    nr_sem,
    ps_sem,
    pr_sem,
):
    g = lax.axis_index("dp")
    t = lax.axis_index("tensor")
    y, z = g // NZ, g % NZ
    x, core = t // 2, t % 2
    yp, ym = (y + 1) % NY, (y + NY - 1) % NY
    zp, zm = (z + 1) % NZ, (z + NZ - 1) % NZ
    xp, xm = (x + 1) % NX, (x + NX - 1) % NX
    dev_yp, dev_ym = (yp * NZ + z, t), (ym * NZ + z, t)
    dev_zp, dev_zm = (y * NZ + zp, t), (y * NZ + zm, t)
    dev_xp, dev_xm = (g, xp * 2 + core), (g, xm * 2 + core)
    dev_c = (g, x * 2 + 1 - core)
    lane_t = pl.multiple_of(t * ROWS, ROWS)
    both_ways = (True, False)

    barrier = pltpu.get_barrier_semaphore()
    z_line = [(y * NZ + (z + k) % NZ, t) for k in range(1, NZ)]
    y_line = [((y + k) % NY * NZ + z, t) for k in range(1, NY)]
    near = z_line + y_line + [dev_xp, dev_xm, dev_c]
    for device in near:
        pl.semaphore_signal(barrier, inc=1, device_id=device, device_id_type=MESH)

    j0 = (5 * x) // 2
    load_g = pltpu.make_async_copy(
        g_hbm.at[:, pl.ds(pl.multiple_of(j0 * BL, BL), SPAN * BL)], gin, load_sem.at[1]
    )
    load_g.start()
    own_x = pltpu.make_async_copy(x_hbm, xall.at[y, z], load_sem.at[0])
    own_x.start()
    later = [
        pltpu.make_async_copy(lr_hbm, lhs.at[:, pl.ds(ROWS, ROWS)], load_sem.at[2]),
        pltpu.make_async_copy(rr_hbm, rr, load_sem.at[3]),
    ]
    load_g.wait()
    sends_g = core == y // 2

    @pl.when(sends_g)
    def _():
        for j in range(SPAN):
            block = gin[:, j * BL : (j + 1) * BL].T
            gsend[:, j * CW : (j + 1) * CW, :] = block.reshape(N_DP, CW, TOK)

    own_x.wait()
    pl.semaphore_wait(barrier, len(near))

    z_off = (0, NZ - 1, 1, NZ - 2, 2, NZ - 3, 3, 4)

    def az(k, right):
        zs = (z + NZ - k) % NZ if right else (z + k) % NZ
        if k < 3:
            rows = pl.ds(0, TA)
        else:
            rows = pl.ds(0, TAH) if right else pl.ds(TAH, TA - TAH)
        ref = xall.at[y, zs, rows]
        n = k * 2 + (0 if right else 1)
        return remote(ref, ref, sent.at[n], az_sem.at[n], dev_zp if right else dev_zm)

    def ay(p, right):
        ref = xall.at[y, (z + z_off[p]) % NZ, pl.ds(0, TA)]
        n = p * 2 + (0 if right else 1)
        return remote(ref, ref, sent.at[8 + n], ay_sem.at[n], dev_yp if right else dev_ym)

    def ay2(p):
        right = p % 2 == 0
        ref = xall.at[ym if right else yp, (z + z_off[p]) % NZ, pl.ds(0, TA)]
        return remote(ref, ref, sent.at[24 + p], ay2_sem.at[p], dev_yp if right else dev_ym)

    def by(k, right):
        if k == 0:
            ys, rows = y, pl.ds(TA, TB)
        elif right:
            ys, rows = ym, pl.ds(TA, TBH)
        else:
            ys, rows = yp, pl.ds(TA + TBH, TB - TBH)
        ref = xall.at[ys, z, rows]
        n = k * 2 + (0 if right else 1)
        return remote(ref, ref, sent.at[32 + n], by_sem.at[n], dev_yp if right else dev_ym)

    def bz(q, k, right):
        ys = (y, ym, yp, (y + 2) % NY)[q]
        zs = (z + NZ - k) % NZ if right else (z + k) % NZ
        if k < 3:
            rows = pl.ds(TA, TB)
        else:
            rows = pl.ds(TA, TBH) if right else pl.ds(TA + TBH, TB - TBH)
        ref = xall.at[ys, zs, rows]
        n = q * 8 + k * 2 + (0 if right else 1)
        return remote(ref, ref, sent.at[36 + n], bz_sem.at[n], dev_zp if right else dev_zm)

    def az_step(k):
        for right in both_ways:
            az(k - 1, right).wait_recv()
            az(k, right).start()
            p = 2 * k - 1 if right else 2 * k
            for way in both_ways:
                ay(p, way).start()

    def bz_step(q, k):
        for right in both_ways:
            if k:
                bz(q, k - 1, right).wait_recv()
            bz(q, k, right).start()

    def ay2_step(p):
        ay(p, p % 2 == 0).wait_recv()
        ay2(p).start()

    for right in both_ways:
        az(0, right).start()
    for right in both_ways:
        by(0, right).start()

    for device in y_line:
        pl.semaphore_signal(greet_sem, inc=1, device_id=device, device_id_type=MESH)

    offset = pl.multiple_of(((5 * x) % 2) * 16, 16)
    gx_rows = pl.ds(pl.multiple_of(x * GX, 16), GX)
    own_lanes = pl.ds(pl.multiple_of(g * TOK, TOK), TOK)

    def send_g(to):
        remote(
            gsend.at[to, pl.ds(offset, GX)], gt.at[gx_rows, own_lanes], gs_sem, gr_sem, (to, t)
        ).start()

    @pl.when(sends_g)
    def _():
        pltpu.make_async_copy(
            gsend.at[g, pl.ds(offset, GX)], gt.at[gx_rows, own_lanes], gr_sem
        ).start()
        for k in range(1, NZ):
            send_g(y * NZ + (z + k) % NZ)

    for right in both_ways:
        ay(0, right).start()
    pl.semaphore_wait(greet_sem, len(y_line))

    def send_g_row(k):
        @pl.when(sends_g)
        def _():
            for n in range(NZ):
                send_g((y + k) % NY * NZ + (z + n) % NZ)

    half_lanes = pl.ds(pl.multiple_of(core * HALF * TOK, HALF * TOK), HALF * TOK)
    other_lanes = pl.ds(pl.multiple_of((1 - core) * HALF * TOK, HALF * TOK), HALF * TOK)

    quarter = HALF * TOK // 2

    def gxc(k, right):
        xs = x if k < 2 else (xm if right else xp)
        first = right if k != 1 else not right
        rows = pl.ds(pl.multiple_of(xs * GX, 16), GX)
        start = core * HALF * TOK + (0 if first else quarter)
        ref = gt.at[rows, pl.ds(pl.multiple_of(start, quarter), quarter)]
        n = k * 2 + (0 if right else 1)
        return remote(ref, ref, sent.at[68 + n], gx_sem.at[n], dev_xp if right else dev_xm)

    def gcc(step):
        rows = pl.ds(pl.multiple_of((x + NX - step) % NX * GX, 16), GX)
        ref = gt.at[rows, half_lanes]
        return remote(ref, ref, sent.at[74 + step], gc_sem.at[step], dev_c)

    def step_by():
        for right in both_ways:
            by(0, right).wait_recv()
        for right in both_ways:
            by(1, right).start()

    def step_by1():
        for right in both_ways:
            by(1, right).wait_recv()

    def step_G0():
        await_bytes(gt.at[gx_rows, half_lanes], gr_sem)
        for k in range(2):
            for right in both_ways:
                gxc(k, right).start()
        gcc(0).start()

    def step_G1():
        for right in both_ways:
            gxc(0, right).wait_recv()
            gxc(2, right).start()
        for right in both_ways:
            gxc(1, right).wait_recv()
            gcc(1 if right else 3).start()

    def step_G2():
        for right in both_ways:
            gxc(2, right).wait_recv()
        gcc(2).start()

    def step_ay7():
        for right in both_ways:
            az(3, right).wait_recv()
        for right in both_ways:
            ay(7, right).start()

    def step_L():
        for copy in later:
            copy.start()

    az_step(1)
    send_g_row(1)
    step_by()
    send_g_row(2)
    az_step(2)
    send_g_row(3)
    bz_step(0, 0)
    ay2_step(0)
    bz_step(1, 0)
    bz_step(2, 0)
    az_step(3)
    step_L()
    ay2_step(1)
    ay2_step(2)
    bz_step(0, 1)
    step_by1()
    bz_step(3, 0)
    step_G0()
    bz_step(1, 1)
    bz_step(2, 1)
    step_ay7()
    ay2_step(3)
    ay2_step(4)
    bz_step(0, 2)
    bz_step(3, 1)
    ay2_step(5)
    ay2_step(6)
    bz_step(1, 2)
    bz_step(2, 2)
    step_G1()
    bz_step(0, 3)
    bz_step(3, 2)
    ay2_step(7)
    bz_step(1, 3)
    bz_step(2, 3)
    bz_step(3, 3)
    step_G2()

    def add_tokens(ys):
        lanes = pl.ds(pl.multiple_of(ys * NZ * TOK, NZ * TOK), NZ * TOK)
        part = xall[ys].reshape(NZ * TOK, NRB * ROWS)
        return jnp.dot(gt[:, lanes], part, preferred_element_type=jnp.float32)

    for step in (0, 1, 3, 2):
        gcc(step).wait_recv()
    for right in both_ways:
        bz(0, 3, right).wait_recv()
    acc[...] = add_tokens(y)
    for p in range(NZ):
        ay(p, p % 2 == 1).wait_recv()
    for q in (1, 2):
        for right in both_ways:
            bz(q, 3, right).wait_recv()
    acc[...] += add_tokens(ym)
    acc[...] += add_tokens(yp)
    for p in range(NZ):
        ay2(p).wait_recv()
    for right in both_ways:
        bz(3, 3, right).wait_recv()
    acc[...] += add_tokens((y + 2) % NY)
    for i in range(NRB):
        for j in range(NCB):
            tiles[i * NCB + j] = acc[
                j * CW : (j + 1) * CW, i * ROWS : (i + 1) * ROWS
            ].astype(jnp.bfloat16)
    tiles[NB] = jnp.zeros((CW, ROWS), jnp.bfloat16)

    bt_rows = pl.ds(pl.multiple_of(g * CW, CW), CW)
    bt_lanes = pl.ds(lane_t, ROWS)
    def listed_block(to, s):
        return listed[s, to]

    def send_blocks(s):
        def send_block(d):
            to = (g + d) % N_DP
            sbuf[s, to] = tiles[listed_block(to, s)]
            remote(
                sbuf.at[s, to], bt.at[s, bt_rows, bt_lanes], ss_sem.at[s], sr_sem.at[s], (to, t)
            ).start()

        sbuf[s, g] = tiles[listed_block(g, s)]
        pltpu.make_async_copy(sbuf.at[s, g], bt.at[s, bt_rows, bt_lanes], sr_sem.at[s]).start()
        for d in range(1, N_DP):
            send_block(d)

    def lanes_of(xs, cs):
        return pl.ds(pl.multiple_of((xs * 2 + cs) * ROWS, ROWS), ROWS)

    def bxc(s, k, right):
        xs = x if k < 2 else (xm if right else xp)
        first = right if k != 1 else not right
        rows = pl.ds(0 if first else BL // 2, BL // 2)
        ref = bt.at[s, rows, lanes_of(xs, core)]
        n = s * 6 + k * 2 + (0 if right else 1)
        return remote(ref, ref, sent.at[78 + n], bx_sem.at[n], dev_xp if right else dev_xm)

    def bcc(s, step):
        ref = bt.at[s, :, lanes_of((x + NX - step) % NX, core)]
        n = s * 4 + step
        return remote(ref, ref, sent.at[90 + n], bc_sem.at[n], dev_c)

    def gather_start(s):
        await_bytes(bt.at[s, :, bt_lanes], sr_sem.at[s])
        for k in range(2):
            for right in both_ways:
                bxc(s, k, right).start()
        bcc(s, 0).start()
        own = bt[s, :, bt_lanes].astype(jnp.float32)
        norms[s, t, 0:8] = jnp.sum((own * own).reshape(-1, 8, ROWS), axis=0)

    def gather_middle(s):
        for right in both_ways:
            bxc(s, 0, right).wait_recv()
            bxc(s, 2, right).start()
        for right in both_ways:
            bxc(s, 1, right).wait_recv()
            bcc(s, 1 if right else 3).start()

    def gather_end(s):
        for right in both_ways:
            bxc(s, 2, right).wait_recv()
        bcc(s, 2).start()
        for step in (0, 1, 3, 2):
            bcc(s, step).wait_recv()

    def norm_copy(s, d):
        ref = norms.at[s, t]
        return remote(ref, ref, nsend_sem.at[s], nr_sem.at[s, d], (g, (t + d) % N_T))

    def precondition(s):
        lhs[s, 0:ROWS] = bt[s, pl.ds(lane_t, ROWS), :]
        both = lax.dot_general(
            lhs[s], bt[s], (((1,), (1,)), ((), ())), preferred_element_type=jnp.float32
        )
        applied = both[ROWS:].astype(jnp.bfloat16)
        precond = jnp.dot(applied, rr[s], preferred_element_type=jnp.float32)
        squares = precond * precond
        folded = jnp.sum(squares.reshape(-1, 8, BL), axis=0)
        total = folded[:, 0:ROWS]
        for m in range(1, BL // ROWS):
            total = total + folded[:, m * ROWS : (m + 1) * ROWS]
        norms[s, t, 8:16] = total
        for d in range(1, N_T):
            norm_copy(s, d).start()
        pre[s] = precond.reshape(ROWS, 8, ROWS).reshape(8 * ROWS, ROWS)
        nr_out[s] = both[0:ROWS]

    def send_rows(s):
        for d in range(1, N_T):
            norm_copy(s, d).wait_recv()
        sums = jnp.sum(norms[s], axis=0)
        grad_sq = jnp.sum(sums[0:8], keepdims=True)
        prec_sq = jnp.sum(sums[8:16], keepdims=True)
        scale = jnp.sqrt(grad_sq) * lax.rsqrt(prec_sq + epsilon)
        pbuf[s] = (pre[s] * scale).reshape(N_DP, 32, ROWS).astype(jnp.bfloat16)
        pltpu.make_async_copy(pbuf.at[s, g], rv.at[s, g], pr_sem.at[s]).start()

        def send_back(d, carry):
            to = (g + d) % N_DP
            remote(pbuf.at[s, to], rv.at[s, g], ps_sem.at[s], pr_sem.at[s], (to, t)).start()
            return carry

        lax.fori_loop(1, N_DP, send_back, 0)

    def left(s):
        own = bt[s, :, bt_lanes]
        nl_out[s] = lax.dot_general(
            own, bt[s], (((0,), (0,)), ((), ())), preferred_element_type=jnp.float32
        )

    send_blocks(0)
    gather_start(0)
    send_blocks(1)
    gather_middle(0)
    gather_start(1)
    for copy in later:
        copy.wait()
    gather_end(0)
    precondition(0)
    gather_middle(1)
    send_rows(0)
    gather_end(1)
    precondition(1)
    left(0)
    left(1)
    send_rows(1)

    for k in range(4):
        for right in both_ways:
            az(k, right).wait_send()
            for q in range(NY):
                bz(q, k, right).wait_send()
    for p in range(NZ):
        for right in both_ways:
            ay(p, right).wait_send()
        ay2(p).wait_send()
    for right in both_ways:
        for k in range(2):
            by(k, right).wait_send()
        for k in range(3):
            gxc(k, right).wait_send()
    for step in range(4):
        gcc(step).wait_send()

    @pl.when(sends_g)
    def _():
        await_bytes(gsend.at[pl.ds(0, N_DP - 1), pl.ds(0, GX)], gs_sem)

    for s in range(2):
        await_bytes(sbuf.at[s, pl.ds(0, N_DP - 1)], ss_sem.at[s])
        for k in range(3):
            for right in both_ways:
                bxc(s, k, right).wait_send()
        for step in range(4):
            bcc(s, step).wait_send()
        await_bytes(norms.at[s, pl.ds(0, N_T - 1)], nsend_sem.at[s])
        await_bytes(pbuf.at[s, pl.ds(0, N_DP - 1)], ps_sem.at[s])

    lane = lax.broadcasted_iota(jnp.int32, (8, ROWS), 1)
    slots = jnp.zeros((8, ROWS), jnp.int32)
    for slot in range(2 * N_DP):
        slots = jnp.where(lane == listed_block(slot % N_DP, slot // N_DP), slot, slots)
    for b in range(NB):
        slot_of[b] = jnp.max(jnp.where(lane == b, slots, 0))

    for s in range(2):
        await_bytes(rv.at[s], pr_sem.at[s])

    for b in range(NB):
        slot = slot_of[b]
        rows = rv[slot // N_DP, slot % N_DP]
        for k in range(4):
            up_out[k, b] = rows[k * 8 : (k + 1) * 8]

def body(
    layer_inputs,
    output_grads,
    left_stats,
    right_stats,
    left_roots,
    right_roots,
    owner_blocks,
    block_counts,
):
    f32, bf16 = jnp.float32, jnp.bfloat16
    live = jnp.arange(2, dtype=jnp.int32)[:, None] < block_counts[None, :]
    listed = jnp.where(live, jnp.clip(owner_blocks.T, 0, NB - 1), NB)
    dma = pltpu.SemaphoreType.DMA
    hbm = pl.BlockSpec(memory_space=pltpu.HBM)
    vmem = pl.BlockSpec(memory_space=pltpu.VMEM)
    smem = pl.BlockSpec(memory_space=pltpu.SMEM)
    left_gram, right_gram, update = pl.pallas_call(
        kernel,
        out_shape=(
            jax.ShapeDtypeStruct((2, ROWS, BL), f32),
            jax.ShapeDtypeStruct((2, ROWS, BL), f32),
            jax.ShapeDtypeStruct((4, NB, 8, ROWS), bf16),
        ),
        in_specs=[hbm] * 4 + [smem],
        out_specs=(vmem, vmem, vmem),
        scratch_shapes=[
            pltpu.VMEM((NY, NZ, TOK, NRB * ROWS), bf16),
            pltpu.VMEM((TOK, SPAN * BL), bf16),
            pltpu.VMEM((N_DP, SPAN * CW, TOK), bf16),
            pltpu.VMEM((GROWS, N_DP * TOK), bf16),
            pltpu.VMEM((GROWS, NRB * ROWS), f32),
            pltpu.VMEM((NB + 1, CW, ROWS), bf16),
            pltpu.VMEM((2, N_DP, CW, ROWS), bf16),
            pltpu.VMEM((2, BL, BL), bf16),
            pltpu.VMEM((2, 2 * ROWS, BL), bf16),
            pltpu.VMEM((2, BL, BL), bf16),
            pltpu.VMEM((2, 8 * ROWS, ROWS), f32),
            pltpu.VMEM((2, N_T, 16, ROWS), f32),
            pltpu.VMEM((2, N_DP, 32, ROWS), bf16),
            pltpu.VMEM((2, N_DP, 32, ROWS), bf16),
            pltpu.SMEM((NB,), jnp.int32),
            dma((4,)),
            pltpu.SemaphoreType.REGULAR,
            dma((98,)),
            dma((8,)),
            dma((16,)),
            dma((8,)),
            dma((4,)),
            dma((32,)),
            dma,
            dma,
            dma((6,)),
            dma((4,)),
            dma((2,)),
            dma((2,)),
            dma((12,)),
            dma((8,)),
            dma((2,)),
            dma((2, N_T)),
            dma((2,)),
            dma((2,)),
        ],
        compiler_params=pltpu.CompilerParams(
            collective_id=0, has_side_effects=True, vmem_limit_bytes=50 * 1024 * 1024
        ),
        cost_estimate=pl.CostEstimate(
            flops=4_000_000_000, bytes_accessed=16_000_000, transcendentals=0
        ),
    )(
        layer_inputs.reshape(TOK, NRB * ROWS),
        output_grads,
        left_roots[0],
        right_roots[0],
        listed,
    )
    update = update.reshape(4, NRB, NCB * BL)
    new_left = decay_rate * left_stats + (1.0 - decay_rate) * left_gram[None]
    new_right = decay_rate * right_stats + (1.0 - decay_rate) * right_gram[None]
    return (new_left, new_right, update)


def solution(mesh):
    placed = (
        P("dp", None, "tensor"),
        P("dp", None),
        P("dp", None, "tensor", None),
        P("dp", None, "tensor", None),
        P("dp", None, "tensor", None),
        P("dp", None, None, None),
        P(),
        P(),
    )
    return jax.shard_map(
        body,
        mesh=mesh,
        in_specs=placed,
        out_specs=(
            P("dp", None, "tensor", None),
            P("dp", None, "tensor", None),
            P(("tensor", "dp"), None, None),
        ),
        check_vma=False,
    )
```
